32 devices in a mesh: row: 8 (over z, y), col: 4 (over x, core).
Axes of the slice: x: 2, y: 2, z: 4, core: 2. Of those that a mesh axis runs over, the one named last changes fastest.
Arguments:
- embedding: bfloat16 [4, 8, 48, 256], P('col', 'row'), may hold values from -0.3984375 to 0.3984375
- preference: float32 [1536], P('row'), may hold values from -2.5 to -0.5
Outputs:
- responsibility: float32 [1536, 1536], P('row', 'col')
- availability: float32 [1536, 1536], P('row', 'col')
The draws below stay inside these ranges and needn't reach their ends.
All inputs are finite; a program needn't handle non-finite values.
Results may differ from the reference program's by a relative error of at most 0.0003.
Values may be sent and summed in bfloat16 or wider, within the bound.
No kernel may reach another device: no remote copies, remote signals or barrier semaphores. Data moves between devices by JAX's collectives and lax.ppermute only.
A program may use at most 64 MiB of HBM per device.

```python
import jax
import jax.numpy as jnp
from jax import lax

E = 256
MOL_DEV = 48
ITERS = 2
N = 1536
N_ROW = 8
N_COL = 4


def block_levels(key, extent, shards, smallest, top_value):
    gain, own = 1.0, jax.random.fold_in(key, 6)
    for dim, shards_of in shards:
        steps = jnp.exp(jax.random.uniform(jax.random.fold_in(own, dim), (shards_of,), jnp.float32, smallest / len(shards), top_value / len(shards)))
        gain = gain * jnp.repeat(steps, extent[dim] // shards_of).reshape([-1 if axis == dim else 1 for axis in range(len(extent))])
    return gain


def noise(key, dims, scale, reach, cuts=(), kind=jnp.bfloat16):
    gain = block_levels(key, dims, cuts, -0.22, 0.18) if cuts else 1.0
    values = jax.random.normal(key, dims, jnp.float32) * scale * gain
    return jnp.minimum(jnp.maximum(values, -reach), reach).astype(kind)


def setup_inputs(seed: int = 0) -> dict:
    keys = jax.random.split(jax.random.key(seed), 3)
    embedding = noise(keys[0], (N_COL, N_ROW, MOL_DEV, E), 0.0625, 0.3984375, ((0, 4), (1, 8)))
    preference = jnp.clip(-2.5 + 2.0 * jax.random.uniform(keys[1], (N,), jnp.float32) ** block_levels(keys[1], (N,), ((0, 8),), -0.2, 0.2), -2.5, -0.5)
    return dict(embedding=embedding, preference=preference)


DAMPING = 0.5


def similarity(row_emb, col_emb, row_start, col_start, pref_rows):
    cross = lax.dot_general(row_emb, col_emb, (((1,), (1,)), ((), ())), preferred_element_type=jnp.float32)
    row_vals = row_emb.astype(jnp.float32)
    col_vals = col_emb.astype(jnp.float32)
    row_sq = jnp.sum(row_vals * row_vals, axis=1)
    col_sq = jnp.sum(col_vals * col_vals, axis=1)
    dist = (2.0 * cross - row_sq[:, None]) - col_sq[None, :]
    row_ids = row_start + jnp.arange(row_emb.shape[0], dtype=jnp.int32)
    col_ids = col_start + jnp.arange(col_emb.shape[0], dtype=jnp.int32)
    diagonal = row_ids[:, None] == col_ids[None, :]
    return jnp.where(diagonal, pref_rows[:, None], dist), diagonal


def top_two(summed):
    first = jnp.max(summed, axis=1)
    hits = summed == first[:, None]
    repeats = jnp.sum(hits.astype(jnp.int32), axis=1)
    others = jnp.max(jnp.where(hits, -jnp.inf, summed), axis=1)
    second = jnp.where(repeats > 1, first, others)
    return first, second


def row_update(sim, avail, resp, first, second):
    summed = avail + sim
    fresh = sim - jnp.where(summed == first[:, None], second[:, None], first[:, None])
    return DAMPING * resp + (1.0 - DAMPING) * fresh


def reference(embedding, preference):
    width = embedding.shape[3]
    flat = embedding.reshape(-1, width)
    total = flat.shape[0]
    block = MOL_DEV * N_COL
    groups = total // block
    row_groups = flat.reshape(groups, block, width)
    pref_groups = preference.reshape(groups, block)
    starts = jnp.arange(groups, dtype=jnp.int32) * block

    def build(items):
        rows, prefs, start = items
        sim_rows, unused = similarity(rows, flat, start, jnp.int32(0), prefs)
        return sim_rows

    sim = lax.map(build, (row_groups, pref_groups, starts))
    ids = jnp.arange(total, dtype=jnp.int32)
    diagonal = ids[:, None] == ids[None, :]
    resp = jnp.zeros((groups, block, total), jnp.float32)
    avail = jnp.zeros((groups, block, total), jnp.float32)

    def update(items):
        sim_rows, avail_rows, resp_rows = items
        first, second = top_two(avail_rows + sim_rows)
        return row_update(sim_rows, avail_rows, resp_rows, first, second)

    for step in range(ITERS):
        resp = lax.map(update, (sim, avail, resp))
        whole = resp.reshape(total, total)
        positive = jnp.where(diagonal, whole, jnp.maximum(whole, 0.0))
        colsum = jnp.sum(positive, axis=0)
        renew = colsum[None, :] - positive
        renew = jnp.where(diagonal, renew, jnp.minimum(renew, 0.0))
        avail = (DAMPING * avail.reshape(total, total) + (1.0 - DAMPING) * renew).reshape(groups, block, total)
    return resp.reshape(total, total), avail.reshape(total, total)
```

```python
import functools
import math

import jax
import jax.numpy as jnp
from jax import lax
from jax.experimental import pallas as pl
from jax.experimental.pallas import tpu as pltpu
from jax.sharding import PartitionSpec as P

ITERS = 2
DAMPING = 0.5
LOW = -1e30


def push(one, two, item):
    return jnp.maximum(one, item), jnp.maximum(two, jnp.minimum(one, item))

def fold(one, two):
    for shift in (4, 2, 1):
        o, t = pltpu.roll(one, shift, 0), pltpu.roll(two, shift, 0)
        one, two = jnp.maximum(one, o), jnp.maximum(jnp.minimum(one, o), jnp.maximum(two, t))
    return one, two

def kernel(rows, cols, win, x_ref, pref_ref, at_ref, resp_ref, avail_ref, g_ref, c_ref, q_ref, row_ref, r_out, a_out, T=256, CH=16, L4=16):
    n, width = x_ref.shape
    def qbody(j, _):
        s = pl.ds(pl.multiple_of(j * 64, 64), 64)
        x = x_ref[s, :].astype(jnp.float32)
        q_ref[s, :] = jnp.broadcast_to(jnp.sum(x * x, axis=1, keepdims=True), (64, 128))
        return 0
    lax.fori_loop(0, n // 64, qbody, 0)
    eye = lax.broadcasted_iota(jnp.int32, (T, T), 0) == lax.broadcasted_iota(jnp.int32, (T, T), 1)
    for t in range(n // T):
        lanes = slice(t * T, (t + 1) * T)
        xt = x_ref[lanes, :] * jnp.bfloat16(2)
        def product(start):
            s = pl.ds(start, T)
            p = lax.dot_general(x_ref[s, :], xt, (((1,), (1,)), ((), ())), preferred_element_type=jnp.float32)
            qq = q_ref[s, :]
            return p, p - jnp.concatenate([qq] * (T // 128), axis=1)
        def take(g, m):
            one, two = m
            for r in range(0, T, 8):
                one, two = push(one, two, g[r:r + 8, :])
            return one, two
        p, g = product(t * T)
        dq = jnp.sum(jnp.where(eye, p, 0.0), axis=0, keepdims=True)
        own = pref_ref[:, lanes] + 0.5 * dq
        g = jnp.where(eye, LOW, g)
        g_ref[lanes, lanes] = g
        m = (jnp.full((8, T), LOW), jnp.full((8, T), LOW))
        m = take(g, m)
        def body(j, m):
            b = j + (j >= t).astype(jnp.int32)
            st = pl.multiple_of(b * T, T)
            p, g = product(st)
            g_ref[pl.ds(st, T), lanes] = g
            return take(g, m)
        m = lax.fori_loop(0, n // T - 1, body, m)
        one, two = fold(*m)
        own = jnp.broadcast_to(own, (8, T))
        one, two = push(one, two, own)
        row_ref[0, :, lanes] = one
        row_ref[1, :, lanes] = 0.25 * (one - two)
        row_ref[2, :, lanes] = own
        row_ref[3, :, lanes] = 0.5 * (own - jnp.where(own == one, two, one))
        row_ref[4, :, lanes] = jnp.zeros((8, T), jnp.float32)
    sub = lax.broadcasted_iota(jnp.int32, (CH, 128), 0)
    lane = lax.broadcasted_iota(jnp.int32, (CH, 128), 1)
    first = row_ref[0]; gain = row_ref[1]
    def body(j, m):
        one, two = m
        st = pl.multiple_of(j * CH, CH)
        s = pl.ds(st, CH)
        lb = pl.ds(pl.multiple_of((j * CH // 128) * 128, 128), 128)
        d = lane - sub == lax.rem(j * CH, 128)
        g = g_ref[s, :]
        w = jnp.concatenate([jnp.where(g[r:r+8] == first, gain, 0.0) for r in range(0, CH, 8)], 0)
        acc = w[:, 0:128]
        for l in range(128, n, 128):
            acc = acc + w[:, l:l + 128]
        diag = jnp.concatenate([row_ref[3, :, lb]] * (CH // 8), 0)
        acc = acc + jnp.where(d, 0.5 * diag, 0.0)
        c = jnp.broadcast_to(jnp.sum(acc, axis=1, keepdims=True), (CH, 128))
        c_ref[s, :] = c
        dd = jnp.where(d, c, 0.0)
        tot = dd[0:8]
        for r in range(8, CH, 8): tot = tot + dd[r:r+8]
        row_ref[4, :, lb] += tot
        u = g + jnp.minimum(jnp.concatenate([c] * (n // 128), 1) - w, 0.0)
        for r in range(0, CH, 8):
            one, two = push(one, two, u[r:r + 8])
        return one, two
    m = lax.fori_loop(0, n // CH, body, (jnp.full((8, n), LOW), jnp.full((8, n), LOW)))
    one, two = fold(*m)
    half = jnp.sum(row_ref[4], axis=0, keepdims=True)
    own = row_ref[2]; r1d = row_ref[3]
    av1d = jnp.broadcast_to(half, (8, n)) - 0.5 * r1d
    own2 = own + av1d
    one, two = push(one, two, own2)
    base = 0.25 * first + 0.5 * one
    z = 0.5 * (one - two)
    r2d = 0.5 * r1d + 0.5 * (own - jnp.where(own2 == one, two, one))
    row_ref[4] = one
    row_ref[5] = base
    row_ref[6] = z
    row_ref[7] = r2d
    row_ref[8] = av1d
    r0 = at_ref[0]; c0 = at_ref[1]
    sub4 = lax.broadcasted_iota(jnp.int32, (L4, 128), 0)
    lane4 = lax.broadcasted_iota(jnp.int32, (L4, 128), 1)
    tile = lambda a, k: jnp.concatenate([a] * k, 0)
    def resp2(g, c, first, gain, one, base, z):
        w = jnp.where(g == first, gain, 0.0)
        t = jnp.minimum(c - w, 0.0)
        return (0.75 * g - base) + (w + jnp.where(g + t == one, z, 0.0)), t
    w0 = pl.multiple_of((r0 // 128) * 128, 128)
    def body4(j, _):
        st = pl.multiple_of(c0 + j * L4, L4)
        s = pl.ds(st, L4)
        lb = pl.ds(pl.multiple_of((st // 128) * 128, 128), 128)
        d = lane4 - sub4 == lax.rem(st, 128)
        c = c_ref[s, :]
        acc = jnp.where(d, tile(row_ref[7, :, lb], L4 // 8), 0.0)
        for l in range(0, n, 128):
            k = slice(l, l + 128)
            f = lambda i: tile(row_ref[i, :, k], L4 // 8)
            r2, _ = resp2(g_ref[s, k], c, f(0), f(1), f(4), f(5), f(6))
            acc = acc + jnp.maximum(r2, 0.0)
        cs = 0.5 * jnp.broadcast_to(jnp.sum(acc, axis=1, keepdims=True), (L4, 128))
        for l in range(0, win, 128):
            lw = pl.ds(w0 + l, 128)
            f = lambda i: tile(row_ref[i, :, lw], L4 // 8)
            r2, t = resp2(g_ref[s, lw], c, f(0), f(1), f(4), f(5), f(6))
            a2 = 0.5 * t + jnp.minimum(cs - 0.5 * jnp.maximum(r2, 0.0), 0.0)
            dg = lane4 + (w0 + l) == sub4 + st
            rd = f(7)
            r2 = jnp.where(dg, rd, r2)
            a2 = jnp.where(dg, 0.5 * f(8) + (cs - 0.5 * rd), a2)
            o = pl.ds(pl.multiple_of(j * L4, L4), L4)
            r_out[o, l:l + 128] = r2
            a_out[o, l:l + 128] = a2
        return 0
    lax.fori_loop(0, cols // L4, body4, 0)
    off = pl.multiple_of(r0 - w0, 8)
    g_ref[0:win, 0:cols] = r_out[...].T
    g_ref[win:2 * win, 0:cols] = a_out[...].T
    resp_ref[...] = g_ref[pl.ds(off, rows), 0:cols]
    avail_ref[...] = g_ref[pl.ds(win + off, rows), 0:cols]

def compute(x, pref, at, rows, cols, **kw):
    n = x.shape[0]
    win = -(-(rows + 128 - math.gcd(rows, 128)) // 128) * 128
    f32 = jnp.float32
    return pl.pallas_call(
        functools.partial(kernel, rows, cols, win, **kw),
        out_shape=[jax.ShapeDtypeStruct((rows, cols), f32)] * 2,
        in_specs=[pl.BlockSpec(memory_space=pltpu.VMEM)] * 2 + [pl.BlockSpec(memory_space=pltpu.SMEM)],
        out_specs=[pl.BlockSpec(memory_space=pltpu.VMEM)] * 2,
        scratch_shapes=[pltpu.VMEM((n, n), f32), pltpu.VMEM((n, 128), f32), pltpu.VMEM((n, 128), f32), pltpu.VMEM((9, 8, n), f32),
                        pltpu.VMEM((cols, win), f32), pltpu.VMEM((cols, win), f32)],
        compiler_params=pltpu.CompilerParams(vmem_limit_bytes=48 << 20),
    )(x, pref, at)


def local(embedding, preference):
    rows_n, cols_n = lax.axis_size("row"), lax.axis_size("col")
    mol, width = embedding.shape[2:]
    total = mol * rows_n * cols_n
    rows, cols = mol * cols_n, mol * rows_n
    if 4 * total * total > 24 << 20:
        return tiled(embedding, preference)
    part = lax.all_gather(embedding.reshape(mol, width), "row", axis=0, tiled=True)
    x = lax.all_gather(part, "col", axis=0, tiled=True)
    pref = lax.all_gather(preference, "row", axis=0, tiled=True).reshape(1, total)
    at = jnp.stack([lax.axis_index("row") * rows, lax.axis_index("col") * cols]).astype(jnp.int32)
    return tuple(compute(x, pref, at, rows, cols))


def broadcast(block, axis, source):
    block = jnp.where(lax.axis_index(axis) == source, block, jnp.zeros_like(block))
    return lax.psum(block, axis)


def similarity(row_emb, col_emb, row_start, col_start, pref_rows):
    cross = lax.dot_general(
        row_emb, col_emb, (((1,), (1,)), ((), ())), preferred_element_type=jnp.float32
    )
    row_vals = row_emb.astype(jnp.float32)
    col_vals = col_emb.astype(jnp.float32)
    row_sq = jnp.sum(row_vals * row_vals, axis=1)
    col_sq = jnp.sum(col_vals * col_vals, axis=1)
    dist = 2.0 * cross - row_sq[:, None] - col_sq[None, :]
    row_ids = row_start + jnp.arange(row_emb.shape[0], dtype=jnp.int32)
    col_ids = col_start + jnp.arange(col_emb.shape[0], dtype=jnp.int32)
    diagonal = row_ids[:, None] == col_ids[None, :]
    return (jnp.where(diagonal, pref_rows[:, None], dist), diagonal)


def top_two(summed):
    first = jnp.max(summed, axis=1)
    hits = summed == first[:, None]
    repeats = jnp.sum(hits.astype(jnp.int32), axis=1)
    others = jnp.max(jnp.where(hits, -jnp.inf, summed), axis=1)
    second = jnp.where(repeats > 1, first, others)
    return (first, second)


def tiled(embedding, preference):
    rows_n = lax.axis_size("row")
    cols_n = lax.axis_size("col")
    row_idx = lax.axis_index("row")
    col_idx = lax.axis_index("col")
    mol = embedding.shape[2]
    width = embedding.shape[3]
    row_count = mol * cols_n
    col_count = mol * rows_n
    column_block = lax.all_gather(embedding, "row", axis=1, tiled=True).reshape(col_count, width)
    offset = row_idx * cols_n % rows_n
    root = row_idx * cols_n // rows_n
    own_slice = lax.dynamic_slice_in_dim(column_block, offset * mol, row_count, 0)
    row_block = broadcast(own_slice, "col", root)
    row_start = row_idx * row_count
    col_start = col_idx * col_count
    sim, diagonal = similarity(row_block, column_block, row_start, col_start, preference)
    resp = jnp.zeros_like(sim)
    avail = jnp.zeros_like(sim)
    for step in range(ITERS):
        summed = avail + sim
        local_first, local_second = top_two(summed)
        firsts, seconds = (
            lax.all_gather(local_first, "col", axis=0, tiled=True),
            lax.all_gather(local_second, "col", axis=0, tiled=True),
        )
        firsts = firsts.reshape(cols_n, row_count)
        seconds = seconds.reshape(cols_n, row_count)
        first = jnp.max(firsts, axis=0)
        at_top = firsts == first[None, :]
        repeats = jnp.sum(at_top.astype(jnp.int32), axis=0)
        others = jnp.max(jnp.where(at_top, -jnp.inf, firsts), axis=0)
        second = jnp.where(repeats > 1, first, jnp.maximum(jnp.max(seconds, axis=0), others))
        fresh = sim - jnp.where(summed == first[:, None], second[:, None], first[:, None])
        resp = DAMPING * resp + (1.0 - DAMPING) * fresh
        positive = jnp.where(diagonal, resp, jnp.maximum(resp, 0.0))
        colsum = lax.psum(jnp.sum(positive, axis=0), "row")
        renew = colsum[None, :] - positive
        renew = jnp.where(diagonal, renew, jnp.minimum(renew, 0.0))
        avail = DAMPING * avail + (1.0 - DAMPING) * renew
    return (resp, avail)


def solution(mesh):
    placed = (P("col", "row", None, None), P("row"))
    return jax.shard_map(
        local,
        mesh=mesh,
        in_specs=placed,
        out_specs=(P("row", "col"), P("row", "col")),
        check_vma=False,
    )
```

```python
import functools
import math

import jax
import jax.numpy as jnp
from jax import lax
from jax.experimental import pallas as pl
from jax.experimental.pallas import tpu as pltpu
from jax.sharding import PartitionSpec as P

ITERS = 2
DAMPING = 0.5
LOW = -1e30
LANES = 128
NT = (((1,), (1,)), ((), ()))
F32, BF16 = jnp.float32, jnp.bfloat16


def push(one, two, item):
    return jnp.maximum(one, item), jnp.maximum(two, jnp.minimum(one, item))


def merge(one, two, o, t):
    return jnp.maximum(one, o), jnp.maximum(jnp.minimum(one, o), jnp.maximum(two, t))


def fold(one, two, at=None):
    for shift in (4, 2, 1):
        o, t = pltpu.roll(one, shift, 0), pltpu.roll(two, shift, 0)
        if at is not None:
            a = pltpu.roll(at, shift, 0)
            at = jnp.where((o > one) | ((o == one) & (a < at)), a, at)
        one, two = merge(one, two, o, t)
    return one, two, at


def thirds(value):
    high = value.astype(BF16).astype(F32)
    rest = value - high
    mid = rest.astype(BF16).astype(F32)
    return high, mid, rest - mid


def squares(x_ref, q_ref, step):
    n, width = x_ref.shape
    ones = jnp.ones((2 * width, LANES), BF16)
    for s in range(0, n, step):
        x = x_ref[s:s + step, :].astype(F32)
        x = x * x
        high = x.astype(BF16)
        low = (x - high.astype(F32)).astype(BF16)
        q_ref[s:s + step, :] = jnp.dot(jnp.concatenate([high, low], 1), ones, preferred_element_type=F32)


def unpack(mesh_n, mol, masks, me, halves, x_ref, pref_ref):
    rows_n, cols_n = mesh_n
    seen = set()
    for half, flip in zip(halves, (0, 1)):
        for p, mask in enumerate(masks):
            owner = me ^ (mask ^ flip)
            row, col = owner // cols_n, owner % cols_n
            at = p * (mol + 8)
            x_ref[pl.ds(pl.multiple_of((col * rows_n + row) * mol, 16), mol), :] = half[at:at + mol, :]
            if (mask ^ flip) // cols_n not in seen:
                seen.add((mask ^ flip) // cols_n)
                tail = half[at + mol:at + mol + 8, :].astype(F32)
                pref_ref[pl.ds(row, 1), :] = (tail[0:1] + tail[1:2]) + tail[2:3]


FIRST, GAIN, OWN, R1D, ONE, TWO, BASE, Z, R2D, AV1D, STAR, WZ = range(12)


def kernel(mesh_n, mol, masks, rows, cols, win, sent_ref, came_ref, resp_ref, avail_ref, x_ref, pref_ref, g_ref, c_ref, q_ref, row_ref, k_ref, r_out, a_out,
           T=512, R=256, CH=128, QS=256):
    n, width = x_ref.shape
    rows_n, cols_n = mesh_n
    row_idx, col_idx = lax.axis_index("row"), lax.axis_index("col")
    unpack(mesh_n, mol, masks, row_idx * cols_n + col_idx, (sent_ref, came_ref), x_ref, pref_ref)
    squares(x_ref, q_ref, QS)
    sub8 = lax.broadcasted_iota(jnp.int32, (8, LANES), 0)
    lane8 = lax.broadcasted_iota(jnp.int32, (8, LANES), 1)
    gap = lane8 - sub8
    pref = jnp.concatenate([pref_ref[r:r + 1, 0:rows] for r in range(rows_n)], 1)
    blocks = n // LANES
    low8 = jnp.full((8, LANES), LOW, F32)
    for t in range(0, n, T):
        xt = x_ref[t:t + T, :] * BF16(2)
        K = T // LANES
        one, two, at = [low8] * K, [low8] * K, [jnp.zeros((8, LANES), jnp.int32)] * K
        dq = [jnp.zeros((8, LANES), F32)] * K
        for b in range(0, n, R):
            p = lax.dot_general(x_ref[b:b + R, :], xt, NT, preferred_element_type=F32)
            for r in range(0, R, 8):
                q = q_ref[b + r:b + r + 8, :]
                for l in range(K):
                    item = p[r:r + 8, l * LANES:(l + 1) * LANES]
                    lo = t + l * LANES
                    on = lo <= b + r < lo + LANES
                    if on:
                        mask = gap == b + r - lo
                        dq[l] = dq[l] + jnp.where(mask, item, 0.0)
                    item = item - q
                    if on:
                        item = jnp.where(mask, LOW, item)
                    g_ref[b + r:b + r + 8, lo:lo + LANES] = item
                    at[l] = jnp.where(item > one[l], b + r, at[l])
                    one[l], two[l] = push(one[l], two[l], item)
        for l in range(K):
            lanes = slice(t + l * LANES, t + (l + 1) * LANES)
            top, next_, a = fold(one[l], two[l], at[l] + sub8)
            own = jnp.broadcast_to(pref[:, lanes] + 0.5 * jnp.sum(dq[l], axis=0, keepdims=True), (8, LANES))
            first, second = push(top, next_, own)
            row_ref[STAR, :, lanes] = top
            row_ref[FIRST, :, lanes] = first
            row_ref[GAIN, :, lanes] = jnp.maximum(0.25 * (top - jnp.maximum(next_, own)), 0.0)
            row_ref[OWN, :, lanes] = own
            row_ref[R1D, :, lanes] = 0.5 * (own - jnp.where(own == first, second, first))
            k_ref[0, :, lanes] = a
            k_ref[1, :, lanes] = a - sub8
            row_ref[ONE, :, lanes] = low8
            row_ref[TWO, :, lanes] = low8
    H = -(-blocks // 16) * 16
    subL = lax.broadcasted_iota(jnp.int32, (LANES, LANES), 0)
    subH = lax.broadcasted_iota(jnp.int32, (H, LANES), 0)
    short, tall = [[], [], []], []
    for l in range(blocks):
        lanes = slice(l * LANES, (l + 1) * LANES)
        k = k_ref[0, 0:1, lanes]
        tall.append(jnp.where(subL == k % LANES, 1.0, 0.0).astype(BF16))
        for i, part in enumerate(thirds(row_ref[GAIN, 0:1, lanes])):
            short[i].append(jnp.where(subH == k // LANES, part, 0.0).astype(BF16))
    tall = jnp.concatenate(tall, 1)
    short = jnp.concatenate([jnp.concatenate(s, 1) for s in short], 0)
    s = lax.dot_general(short, tall, NT, preferred_element_type=F32)
    s = (s[0:H] + s[H:2 * H]) + s[2 * H:]
    half = []
    for l in range(blocks):
        lanes = slice(l * LANES, (l + 1) * LANES)
        av = s[l:l + 1, :]
        row_ref[AV1D, :, lanes] = jnp.broadcast_to(av, (8, LANES))
        half.append(av + 0.5 * row_ref[R1D, 0:1, lanes])
    half = jnp.concatenate(half + [jnp.zeros((H - blocks, LANES), F32)] * (H > blocks), 0)
    half = jnp.concatenate(thirds(half), 0)
    got = jnp.dot(half.astype(BF16), tall, preferred_element_type=F32)
    got = (got[0:H] + got[H:2 * H]) + got[2 * H:]
    pick = lax.broadcasted_iota(jnp.int32, (3 * H, n), 0) % H == lax.broadcasted_iota(jnp.int32, (3 * H, n), 1) // LANES
    side = jnp.concatenate([half, jnp.zeros((LANES - 3 * H, LANES), F32)], 0).T[:, 0:3 * H].astype(BF16)
    c_ref[...] = jnp.dot(side, jnp.where(pick, 1.0, 0.0).astype(BF16), preferred_element_type=F32)
    for l in range(blocks):
        lanes = slice(l * LANES, (l + 1) * LANES)
        k = k_ref[0, 0:1, lanes]
        c = jnp.sum(jnp.where(subH == k // LANES, got[:, lanes], 0.0), axis=0, keepdims=True)
        row_ref[WZ, :, lanes] = jnp.broadcast_to(c, (8, LANES))
    def tops(j, _):
        groups = CH // 8
        a = [jnp.minimum(c_ref[8 * r:8 * r + 8, pl.ds(pl.multiple_of(j * LANES, LANES), LANES)], 0.0) for r in range(groups)]
        at = [pl.ds(pl.multiple_of(j * CH + 8 * r, 8), 8) for r in range(groups)]
        for l in range(blocks):
            k = slice(l * LANES, (l + 1) * LANES)
            star = k_ref[1, :, k] - j * CH
            one, two = row_ref[ONE, :, k], row_ref[TWO, :, k]
            for r in range(groups):
                one, two = push(one, two, jnp.where(star == 8 * r, LOW, g_ref[at[r], k] + a[r]))
            row_ref[ONE, :, k] = one
            row_ref[TWO, :, k] = two
        return 0
    lax.fori_loop(0, n // CH, tops, 0)
    for l in range(blocks):
        k = slice(l * LANES, (l + 1) * LANES)
        one, two, _ = fold(row_ref[ONE, :, k], row_ref[TWO, :, k])
        own, r1d, first, gain, av1d = (row_ref[i, :, k] for i in (OWN, R1D, FIRST, GAIN, AV1D))
        t = jnp.minimum(row_ref[WZ, :, k] - gain, 0.0)
        star = row_ref[STAR, :, k] + t
        own2 = own + av1d
        one, two = push(one, two, star)
        one, two = push(one, two, own2)
        z = (2 / 3) * (one - two)
        row_ref[ONE, :, k] = one
        row_ref[BASE, :, k] = (first + 2.0 * one) * (1 / 3)
        row_ref[Z, :, k] = z
        row_ref[R2D, :, k] = 0.5 * r1d + 0.5 * (own - jnp.where(own2 == one, two, one))
        row_ref[WZ, :, k] = (4 / 3) * gain + jnp.where(star == one, z, 0.0)
        row_ref[STAR, :, k] = t
    r0, c0 = row_idx * rows, col_idx * cols
    w0 = pl.multiple_of((r0 // LANES) * LANES, LANES)
    def body4(j, _):
        st = pl.multiple_of(c0 + j * LANES, LANES)
        groups = LANES // 8
        at = [pl.ds(pl.multiple_of(st + 8 * r, 8), 8) for r in range(groups)]
        out = [pl.ds(pl.multiple_of(j * LANES + 8 * r, 8), 8) for r in range(groups)]
        c = [c_ref[8 * r:8 * r + 8, pl.ds(st, LANES)] for r in range(groups)]
        a = [jnp.minimum(v, 0.0) for v in c]
        r2d = (4 / 3) * row_ref[R2D, :, pl.ds(st, LANES)]
        acc = [jnp.where(gap == 8 * r, r2d, 0.0) for r in range(groups)]
        def resp2(r, k, star, row):
            g = g_ref[at[r], k]
            more = jnp.where(g + a[r] == row[0], row[2], 0.0)
            return (g - row[1]) + jnp.where(star == 8 * r, row[3], more)
        for l in range(blocks):
            k = slice(l * LANES, (l + 1) * LANES)
            star = k_ref[1, :, k] - st
            row = [row_ref[i, :, k] for i in (ONE, BASE, Z, WZ)]
            for r in range(groups):
                acc[r] = acc[r] + jnp.maximum(resp2(r, k, star, row), 0.0)
        cs = [0.375 * jnp.broadcast_to(jnp.sum(v, axis=1, keepdims=True), (8, LANES)) for v in acc]
        for l in range(0, win, LANES):
            k = pl.ds(pl.multiple_of(w0 + l, LANES), LANES)
            star = k_ref[1, :, k] - st
            row = [row_ref[i, :, k] for i in (ONE, BASE, Z, WZ)]
            rd, ad, ts = row_ref[R2D, :, k], row_ref[AV1D, :, k], row_ref[STAR, :, k]
            for r in range(groups):
                r2 = 0.75 * resp2(r, k, star, row)
                t = jnp.where(star == 8 * r, ts, a[r])
                a2 = 0.5 * t + jnp.minimum(cs[r] - 0.5 * jnp.maximum(r2, 0.0), 0.0)
                dg = gap == st + 8 * r - (w0 + l)
                r_out[out[r], l:l + LANES] = jnp.where(dg, rd, r2)
                a_out[out[r], l:l + LANES] = jnp.where(dg, 0.5 * ad + (cs[r] - 0.5 * rd), a2)
        return 0
    lax.fori_loop(0, cols // LANES, body4, 0)
    off = pl.multiple_of(r0 - w0, 8)
    g_ref[0:win, 0:cols] = r_out[...].T
    g_ref[win:2 * win, 0:cols] = a_out[...].T
    resp_ref[...] = g_ref[pl.ds(off, rows), 0:cols]
    avail_ref[...] = g_ref[pl.ds(win + off, rows), 0:cols]


def compute(sent, came, mesh_n, mol, masks, rows, cols):
    n, width = mol * mesh_n[0] * mesh_n[1], sent.shape[1]
    win = -(-(rows + LANES - math.gcd(rows, LANES)) // LANES) * LANES
    return pl.pallas_call(
        functools.partial(kernel, mesh_n, mol, masks, rows, cols, win),
        out_shape=[jax.ShapeDtypeStruct((rows, cols), F32)] * 2,
        in_specs=[pl.BlockSpec(memory_space=pltpu.VMEM)] * 2,
        out_specs=[pl.BlockSpec(memory_space=pltpu.VMEM)] * 2,
        scratch_shapes=[
            pltpu.VMEM((n, width), BF16),
            pltpu.VMEM((mesh_n[0], width), F32),
            pltpu.VMEM((n, n), F32),
            pltpu.VMEM((LANES, n), F32),
            pltpu.VMEM((n, LANES), F32),
            pltpu.VMEM((12, 8, n), F32),
            pltpu.VMEM((2, 8, n), jnp.int32),
            pltpu.VMEM((cols, win), F32),
            pltpu.VMEM((cols, win), F32),
        ],
        compiler_params=pltpu.CompilerParams(vmem_limit_bytes=40 << 20),
    )(sent, came)


def fits(rows_n, cols_n, mol, width):
    n = mol * rows_n * cols_n
    two = rows_n >= 2 and cols_n >= 2 and not rows_n & (rows_n - 1) and not cols_n & (cols_n - 1)
    return (two and 4 * n * n <= 24 << 20 and n % 512 == 0 and mol * rows_n % LANES == 0 and mol % 16 == 0
            and mol * cols_n <= width and width % LANES == 0)


def replicated(embedding, preference):
    rows_n, cols_n = lax.axis_size("row"), lax.axis_size("col")
    mol, width = embedding.shape[2:]
    rows, cols = mol * cols_n, mol * rows_n
    high = lax.reduce_precision(preference, 8, 7)
    mid = lax.reduce_precision(preference - high, 8, 7)
    tail = jnp.stack([high, mid, (preference - high) - mid]).astype(BF16)
    tail = jnp.pad(tail, ((0, 5), (0, width - rows)))
    held = jnp.concatenate([embedding.reshape(mol, width), tail], 0)
    masks = [0]
    for stage in stages(rows_n, cols_n):
        came = [lax.ppermute(held, ("row", "col"), [(i, i ^ m) for i in range(rows_n * cols_n)]) for m in stage]
        if len(masks) * 2 == rows_n * cols_n:
            break
        masks = masks + [m ^ a for m in stage for a in masks]
        held = jnp.concatenate([held] + came, 0)
    return tuple(compute(held, came[0], (rows_n, cols_n), mol, masks, rows, cols))


def stages(rows_n, cols_n):
    far = [m * 2 * cols_n + 1 for m in range(rows_n // 2 - 1, 0, -1)]
    near = [m * 2 + 1 for m in range(cols_n - 1, 0, -1)]
    return ([far] if far else []) + [near, [1]]


def local(embedding, preference):
    if fits(lax.axis_size("row"), lax.axis_size("col"), *embedding.shape[2:]):
        return replicated(embedding, preference)
    return tiled(embedding, preference)


def broadcast(block, axis, source):
    block = jnp.where(lax.axis_index(axis) == source, block, jnp.zeros_like(block))
    return lax.psum(block, axis)


def similarity(row_emb, col_emb, row_start, col_start, pref_rows):
    cross = lax.dot_general(
        row_emb, col_emb, (((1,), (1,)), ((), ())), preferred_element_type=jnp.float32
    )
    row_vals = row_emb.astype(jnp.float32)
    col_vals = col_emb.astype(jnp.float32)
    row_sq = jnp.sum(row_vals * row_vals, axis=1)
    col_sq = jnp.sum(col_vals * col_vals, axis=1)
    dist = 2.0 * cross - row_sq[:, None] - col_sq[None, :]
    row_ids = row_start + jnp.arange(row_emb.shape[0], dtype=jnp.int32)
    col_ids = col_start + jnp.arange(col_emb.shape[0], dtype=jnp.int32)
    diagonal = row_ids[:, None] == col_ids[None, :]
    return (jnp.where(diagonal, pref_rows[:, None], dist), diagonal)


def top_two(summed):
    first = jnp.max(summed, axis=1)
    hits = summed == first[:, None]
    repeats = jnp.sum(hits.astype(jnp.int32), axis=1)
    others = jnp.max(jnp.where(hits, -jnp.inf, summed), axis=1)
    second = jnp.where(repeats > 1, first, others)
    return (first, second)


def tiled(embedding, preference):
    rows_n = lax.axis_size("row")
    cols_n = lax.axis_size("col")
    row_idx = lax.axis_index("row")
    col_idx = lax.axis_index("col")
    mol = embedding.shape[2]
    width = embedding.shape[3]
    row_count = mol * cols_n
    col_count = mol * rows_n
    column_block = lax.all_gather(embedding, "row", axis=1, tiled=True).reshape(col_count, width)
    offset = row_idx * cols_n % rows_n
    root = row_idx * cols_n // rows_n
    own_slice = lax.dynamic_slice_in_dim(column_block, offset * mol, row_count, 0)
    row_block = broadcast(own_slice, "col", root)
    row_start = row_idx * row_count
    col_start = col_idx * col_count
    sim, diagonal = similarity(row_block, column_block, row_start, col_start, preference)
    resp = jnp.zeros_like(sim)
    avail = jnp.zeros_like(sim)
    for step in range(ITERS):
        summed = avail + sim
        local_first, local_second = top_two(summed)
        firsts, seconds = (
            lax.all_gather(local_first, "col", axis=0, tiled=True),
            lax.all_gather(local_second, "col", axis=0, tiled=True),
        )
        firsts = firsts.reshape(cols_n, row_count)
        seconds = seconds.reshape(cols_n, row_count)
        first = jnp.max(firsts, axis=0)
        at_top = firsts == first[None, :]
        repeats = jnp.sum(at_top.astype(jnp.int32), axis=0)
        others = jnp.max(jnp.where(at_top, -jnp.inf, firsts), axis=0)
        second = jnp.where(repeats > 1, first, jnp.maximum(jnp.max(seconds, axis=0), others))
        fresh = sim - jnp.where(summed == first[:, None], second[:, None], first[:, None])
        resp = DAMPING * resp + (1.0 - DAMPING) * fresh
        positive = jnp.where(diagonal, resp, jnp.maximum(resp, 0.0))
        colsum = lax.psum(jnp.sum(positive, axis=0), "row")
        renew = colsum[None, :] - positive
        renew = jnp.where(diagonal, renew, jnp.minimum(renew, 0.0))
        avail = DAMPING * avail + (1.0 - DAMPING) * renew
    return (resp, avail)


def solution(mesh):
    placed = (P("col", "row", None, None), P("row"))
    return jax.shard_map(
        local,
        mesh=mesh,
        in_specs=placed,
        out_specs=(P("row", "col"), P("row", "col")),
        check_vma=False,
    )
```

```python
import functools
import math

import jax
import jax.numpy as jnp
from jax import lax
from jax.experimental import pallas as pl
from jax.experimental.pallas import tpu as pltpu
from jax.sharding import PartitionSpec as P

ITERS = 2
DAMPING = 0.5
LOW = -1e30
LANES = 128
NT = (((1,), (1,)), ((), ()))
F32, BF16 = jnp.float32, jnp.bfloat16


def push(one, two, item):
    return jnp.maximum(one, item), jnp.maximum(two, jnp.minimum(one, item))


def merge(one, two, o, t):
    return jnp.maximum(one, o), jnp.maximum(jnp.minimum(one, o), jnp.maximum(two, t))


def fold(one, two, at=None):
    for shift in (4, 2, 1):
        o, t = pltpu.roll(one, shift, 0), pltpu.roll(two, shift, 0)
        if at is not None:
            a = pltpu.roll(at, shift, 0)
            at = jnp.where((o > one) | ((o == one) & (a < at)), a, at)
        one, two = merge(one, two, o, t)
    return one, two, at


def thirds(value):
    high = value.astype(BF16).astype(F32)
    rest = value - high
    mid = rest.astype(BF16).astype(F32)
    return high, mid, rest - mid


def squares(x_ref, q_ref, step):
    n, width = x_ref.shape
    ones = jnp.ones((2 * width, LANES), BF16)
    for s in range(0, n, step):
        x = x_ref[s:s + step, :].astype(F32)
        x = x * x
        high = x.astype(BF16)
        low = (x - high.astype(F32)).astype(BF16)
        q_ref[s:s + step, :] = jnp.dot(jnp.concatenate([high, low], 1), ones, preferred_element_type=F32)


def unpack(mesh_n, mol, owners, me, pieces, x_ref, pref_ref):
    rows_n, cols_n = mesh_n
    seen = set()
    for piece, masks in zip(pieces, owners):
        for p, mask in enumerate(masks):
            owner = me ^ mask
            row, col = owner // cols_n, owner % cols_n
            at = p * (mol + 8)
            x_ref[pl.ds(pl.multiple_of((col * rows_n + row) * mol, 16), mol), :] = piece[at:at + mol, :]
            if mask // cols_n not in seen:
                seen.add(mask // cols_n)
                tail = piece[at + mol:at + mol + 8, :].astype(F32)
                pref_ref[pl.ds(row, 1), :] = (tail[0:1] + tail[1:2]) + tail[2:3]


FIRST, GAIN, OWN, R1D, ONE, TWO, BASE, Z, R2D, AV1D, STAR, WZ = range(12)


def kernel(mesh_n, mol, owners, rows, cols, win, *refs, T=512, R=256, QS=256):
    pieces, refs = refs[:len(owners)], refs[len(owners):]
    resp_ref, avail_ref, x_ref, pref_ref, g_ref, c_ref, a_ref, q_ref, row_ref, k_ref, r_out, a_out, t_ref, out_sem = refs
    n, width = x_ref.shape
    rows_n, cols_n = mesh_n
    row_idx, col_idx = lax.axis_index("row"), lax.axis_index("col")
    unpack(mesh_n, mol, owners, row_idx * cols_n + col_idx, pieces, x_ref, pref_ref)
    squares(x_ref, q_ref, QS)
    sub8 = lax.broadcasted_iota(jnp.int32, (8, LANES), 0)
    lane8 = lax.broadcasted_iota(jnp.int32, (8, LANES), 1)
    gap = lane8 - sub8
    pref = jnp.concatenate([pref_ref[r:r + 1, 0:rows] for r in range(rows_n)], 1)
    blocks = n // LANES
    low8 = jnp.full((8, LANES), LOW, F32)
    for t in range(0, n, T):
        xt = x_ref[t:t + T, :] * BF16(2)
        K = T // LANES
        one, two, at = [low8] * K, [low8] * K, [jnp.zeros((8, LANES), jnp.int32)] * K
        dq = [jnp.zeros((8, LANES), F32)] * K
        for b in range(0, n, R):
            p = lax.dot_general(x_ref[b:b + R, :], xt, NT, preferred_element_type=F32)
            for r in range(0, R, 8):
                q = q_ref[b + r:b + r + 8, :]
                for l in range(K):
                    item = p[r:r + 8, l * LANES:(l + 1) * LANES]
                    lo = t + l * LANES
                    on = lo <= b + r < lo + LANES
                    if on:
                        mask = gap == b + r - lo
                        dq[l] = dq[l] + jnp.where(mask, item, 0.0)
                    item = item - q
                    if on:
                        item = jnp.where(mask, LOW, item)
                    g_ref[b + r:b + r + 8, lo:lo + LANES] = item
                    at[l] = jnp.where(item > one[l], b + r, at[l])
                    one[l], two[l] = push(one[l], two[l], item)
        for l in range(K):
            lanes = slice(t + l * LANES, t + (l + 1) * LANES)
            top, next_, a = fold(one[l], two[l], at[l] + sub8)
            own = jnp.broadcast_to(pref[:, lanes] + 0.5 * jnp.sum(dq[l], axis=0, keepdims=True), (8, LANES))
            first, second = push(top, next_, own)
            row_ref[STAR, :, lanes] = top
            row_ref[FIRST, :, lanes] = first
            row_ref[GAIN, :, lanes] = jnp.maximum(0.25 * (top - jnp.maximum(next_, own)), 0.0)
            row_ref[OWN, :, lanes] = own
            row_ref[R1D, :, lanes] = 0.5 * (own - jnp.where(own == first, second, first))
            k_ref[0, :, lanes] = a
            k_ref[1, :, lanes] = a - sub8
    H = -(-blocks // 16) * 16
    subL = lax.broadcasted_iota(jnp.int32, (LANES, LANES), 0)
    subH = lax.broadcasted_iota(jnp.int32, (H, LANES), 0)
    short, diag, tall, eyes = [[], [], []], [[], [], []], [], []
    eye = jnp.where(subL == lax.broadcasted_iota(jnp.int32, (LANES, LANES), 1), 1.0, 0.0).astype(BF16)
    for l in range(blocks):
        lanes = slice(l * LANES, (l + 1) * LANES)
        k = k_ref[0, 0:1, lanes]
        eyes.append(eye)
        for i, part in enumerate(thirds(0.5 * row_ref[R1D, 0:1, lanes])):
            diag[i].append(jnp.where(subH == l, part, 0.0).astype(BF16))
        tall.append(jnp.where(subL == k % LANES, 1.0, 0.0).astype(BF16))
        for i, part in enumerate(thirds(row_ref[GAIN, 0:1, lanes])):
            short[i].append(jnp.where(subH == k // LANES, part, 0.0).astype(BF16))
    tall, eyes = jnp.concatenate(tall, 1), jnp.concatenate(eyes, 1)
    short = jnp.concatenate([jnp.concatenate(s, 1) for s in short], 0)
    diag = jnp.concatenate([jnp.concatenate(s, 1) for s in diag], 0)
    s = lax.dot_general(short, tall, NT, preferred_element_type=F32)
    s = (s[0:H] + s[H:2 * H]) + s[2 * H:]
    side = lax.dot_general(jnp.concatenate([tall, eyes], 1), jnp.concatenate([short, diag], 1), NT, preferred_element_type=F32)
    side = (side[:, 0:H] + side[:, H:2 * H]) + side[:, 2 * H:]
    half = []
    for l in range(blocks):
        lanes = slice(l * LANES, (l + 1) * LANES)
        c = jnp.broadcast_to(side[:, l:l + 1], (LANES, LANES))
        c_ref[:, lanes] = c
        a_ref[:, lanes] = jnp.minimum(c, 0.0)
        av = s[l:l + 1, :]
        row_ref[AV1D, :, lanes] = jnp.broadcast_to(av, (8, LANES))
        half.append(av + 0.5 * row_ref[R1D, 0:1, lanes])
    half = jnp.concatenate(half + [jnp.zeros((H - blocks, LANES), F32)] * (H > blocks), 0)
    half = jnp.concatenate(thirds(half), 0).astype(BF16)
    got = jnp.dot(half, tall, preferred_element_type=F32)
    got = (got[0:H] + got[H:2 * H]) + got[2 * H:]
    for l in range(blocks):
        lanes = slice(l * LANES, (l + 1) * LANES)
        k = k_ref[0, 0:1, lanes]
        c = jnp.sum(jnp.where(subH == k // LANES, got[:, lanes], 0.0), axis=0, keepdims=True)
        row_ref[WZ, :, lanes] = jnp.broadcast_to(c, (8, LANES))
    for t in range(0, n, T):
        K = T // LANES
        lanes = [slice(t + l * LANES, t + (l + 1) * LANES) for l in range(K)]
        star = [k_ref[1, :, k] for k in lanes]
        def tops(j, tops):
            one, two = list(tops[:K]), list(tops[K:])
            base = pl.multiple_of(j * LANES, LANES)
            near = [s - base for s in star]
            for r in range(0, LANES, 8):
                a = a_ref[r:r + 8, pl.ds(base, LANES)]
                for l, k in enumerate(lanes):
                    u = jnp.where(near[l] == r, LOW, g_ref[pl.ds(pl.multiple_of(base + r, 8), 8), k] + a)
                    one[l], two[l] = push(one[l], two[l], u)
            return one + two
        ends = lax.fori_loop(0, blocks, tops, [low8] * (2 * K))
        for l, k in enumerate(lanes):
            row_ref[ONE, :, k], row_ref[TWO, :, k], _ = fold(ends[l], ends[K + l])
    for l in range(blocks):
        k = slice(l * LANES, (l + 1) * LANES)
        one, two = row_ref[ONE, :, k], row_ref[TWO, :, k]
        own, r1d, first, gain, av1d = (row_ref[i, :, k] for i in (OWN, R1D, FIRST, GAIN, AV1D))
        t = jnp.minimum(row_ref[WZ, :, k] - gain, 0.0)
        star = row_ref[STAR, :, k] + t
        own2 = own + av1d
        one, two = push(one, two, star)
        one, two = push(one, two, own2)
        z = (2 / 3) * (one - two)
        row_ref[ONE, :, k] = one
        row_ref[BASE, :, k] = (first + 2.0 * one) * (1 / 3)
        row_ref[Z, :, k] = z
        row_ref[R2D, :, k] = 0.5 * r1d + 0.5 * (own - jnp.where(own2 == one, two, one))
        row_ref[WZ, :, k] = (4 / 3) * gain + jnp.where(star == one, z, 0.0)
        row_ref[STAR, :, k] = t
    r0, c0 = row_idx * rows, col_idx * cols
    off = pl.multiple_of(r0 % LANES, 8)
    w0 = pl.multiple_of((r0 // LANES) * LANES, LANES)
    def block(j):
        st = pl.multiple_of(c0 + j * LANES, LANES)
        groups = LANES // 8
        at = [pl.ds(pl.multiple_of(st + 8 * r, 8), 8) for r in range(groups)]
        a = [a_ref[8 * r:8 * r + 8, pl.ds(st, LANES)] for r in range(groups)]
        r2d = (4 / 3) * row_ref[R2D, :, pl.ds(st, LANES)]
        acc = [jnp.where(gap == 8 * r, r2d, 0.0) for r in range(groups)]
        def resp2(r, k, star, row):
            g = g_ref[at[r], k]
            more = jnp.where(g + a[r] == row[0], row[2], 0.0)
            return (g - row[1]) + jnp.where(star == 8 * r, row[3], more)
        for l in range(blocks):
            k = slice(l * LANES, (l + 1) * LANES)
            star = k_ref[1, :, k] - st
            row = [row_ref[i, :, k] for i in (ONE, BASE, Z, WZ)]
            for r in range(groups):
                acc[r] = acc[r] + jnp.maximum(resp2(r, k, star, row), 0.0)
        cs = [0.375 * jnp.broadcast_to(jnp.sum(v, axis=1, keepdims=True), (8, LANES)) for v in acc]
        for l in range(0, win, LANES):
            k = pl.ds(pl.multiple_of(w0 + l, LANES), LANES)
            star = k_ref[1, :, k] - st
            row = [row_ref[i, :, k] for i in (ONE, BASE, Z, WZ)]
            rd, ad, ts = row_ref[R2D, :, k], row_ref[AV1D, :, k], row_ref[STAR, :, k]
            for r in range(groups):
                r2 = 0.75 * resp2(r, k, star, row)
                t = jnp.where(star == 8 * r, ts, a[r])
                a2 = 0.5 * t + jnp.minimum(cs[r] - 0.5 * jnp.maximum(r2, 0.0), 0.0)
                dg = gap == st + 8 * r - (w0 + l)
                r_out[8 * r:8 * r + 8, j * win + l:j * win + l + LANES] = jnp.where(dg, rd, r2)
                a_out[8 * r:8 * r + 8, j * win + l:j * win + l + LANES] = jnp.where(dg, 0.5 * ad + (cs[r] - 0.5 * rd), a2)
        lanes = slice(j * LANES, (j + 1) * LANES)
        for i, (tile, out_ref) in enumerate(((r_out, resp_ref), (a_out, avail_ref))):
            t_ref[i, :, lanes] = tile[:, j * win:(j + 1) * win].T
            copy = pltpu.make_async_copy(t_ref.at[i, pl.ds(off, rows), lanes], out_ref.at[:, lanes], out_sem.at[j, i])
            copy.start()
            copies.append(copy)
    copies = []
    for j in range(cols // LANES):
        block(j)
    for copy in copies:
        copy.wait()


def compute(pieces, mesh_n, mol, owners, rows, cols):
    n, width = mol * mesh_n[0] * mesh_n[1], pieces[0].shape[1]
    win = -(-(rows + LANES - math.gcd(rows, LANES)) // LANES) * LANES
    return pl.pallas_call(
        functools.partial(kernel, mesh_n, mol, owners, rows, cols, win),
        out_shape=[jax.ShapeDtypeStruct((rows, cols), F32)] * 2,
        in_specs=[pl.BlockSpec(memory_space=pltpu.VMEM)] * len(pieces),
        out_specs=[pl.BlockSpec(memory_space=pl.ANY)] * 2,
        scratch_shapes=[
            pltpu.VMEM((n, width), BF16),
            pltpu.VMEM((mesh_n[0], width), F32),
            pltpu.VMEM((n, n), F32),
            pltpu.VMEM((LANES, n), F32),
            pltpu.VMEM((LANES, n), F32),
            pltpu.VMEM((n, LANES), F32),
            pltpu.VMEM((12, 8, n), F32),
            pltpu.VMEM((2, 8, n), jnp.int32),
            pltpu.VMEM((LANES, cols // LANES * win), F32),
            pltpu.VMEM((LANES, cols // LANES * win), F32),
            pltpu.VMEM((2, win, cols), F32),
            pltpu.SemaphoreType.DMA((cols // LANES, 2)),
        ],
        compiler_params=pltpu.CompilerParams(vmem_limit_bytes=40 << 20),
    )(*pieces)


def pack_kernel(mol, embedding_ref, preference_ref, out_ref, e_ref, p_ref, sems):
    copies = [
        pltpu.make_async_copy(preference_ref, p_ref, sems.at[0]),
        pltpu.make_async_copy(embedding_ref, e_ref, sems.at[1]),
    ]
    for copy in copies:
        copy.start()
    for copy in copies:
        copy.wait()
    out_ref[0:mol, :] = e_ref[...]
    values = p_ref[...]
    fill = jnp.zeros((1, out_ref.shape[1] - values.shape[1]), F32)
    parts = [jnp.concatenate([part, fill], 1) for part in thirds(values)]
    out_ref[mol:mol + 8, :] = jnp.concatenate(parts + [jnp.zeros((5, out_ref.shape[1]), F32)], 0).astype(BF16)


def pack(embedding, preference):
    mol, width = embedding.shape
    return pl.pallas_call(
        functools.partial(pack_kernel, mol),
        out_shape=pltpu.VMEM((mol + 8, width), BF16),
        in_specs=[pl.BlockSpec(memory_space=pltpu.HBM)] * 2,
        out_specs=pl.BlockSpec(memory_space=pltpu.VMEM),
        scratch_shapes=[pltpu.VMEM((mol, width), BF16), pltpu.VMEM(preference.shape, F32), pltpu.SemaphoreType.DMA((2,))],
        compiler_params=pltpu.CompilerParams(vmem_limit_bytes=60 << 20),
    )(embedding, preference)


def fits(rows_n, cols_n, mol, width):
    n = mol * rows_n * cols_n
    two = rows_n >= 2 and cols_n >= 2 and not rows_n & (rows_n - 1) and not cols_n & (cols_n - 1)
    return (two and 4 * n * n <= 16 << 20 and n % 512 == 0 and mol * rows_n % LANES == 0 and mol % 16 == 0
            and mol * cols_n <= width and width % LANES == 0)


def stages(rows_n, cols_n):
    far = [m * 2 * cols_n + 1 for m in range(1,rows_n//2)]
    near = [m * 2 + 1 for m in range(1,cols_n)]
    return far, near


def swap(block, mask):
    size = lax.axis_size("row") * lax.axis_size("col")
    return lax.ppermute(block, ("row", "col"), [(i, i ^ mask) for i in range(size)])


def replicated(embedding, preference):
    rows_n, cols_n = lax.axis_size("row"), lax.axis_size("col")
    mol, width = embedding.shape[2:]
    rows, cols = mol * cols_n, mol * rows_n
    held = pack(embedding.reshape(mol, width), preference.reshape(1, rows))
    far, near = stages(rows_n, cols_n)
    line = jnp.concatenate([held] + [swap(held, m) for m in far], 0)
    pieces = [line] + [swap(line, m) for m in near]
    owners = [[n ^ f for f in [0] + far] for n in [0] + near]
    pieces = pieces + [swap(piece, 1) for piece in pieces]
    owners = owners + [[m ^ 1 for m in masks] for masks in owners]
    return tuple(compute(pieces, (rows_n, cols_n), mol, owners, rows, cols))


def local(embedding, preference):
    if fits(lax.axis_size("row"), lax.axis_size("col"), *embedding.shape[2:]):
        return replicated(embedding, preference)
    return tiled(embedding, preference)


def broadcast(block, axis, source):
    block = jnp.where(lax.axis_index(axis) == source, block, jnp.zeros_like(block))
    return lax.psum(block, axis)


def similarity(row_emb, col_emb, row_start, col_start, pref_rows):
    cross = lax.dot_general(
        row_emb, col_emb, (((1,), (1,)), ((), ())), preferred_element_type=jnp.float32
    )
    row_vals = row_emb.astype(jnp.float32)
    col_vals = col_emb.astype(jnp.float32)
    row_sq = jnp.sum(row_vals * row_vals, axis=1)
    col_sq = jnp.sum(col_vals * col_vals, axis=1)
    dist = 2.0 * cross - row_sq[:, None] - col_sq[None, :]
    row_ids = row_start + jnp.arange(row_emb.shape[0], dtype=jnp.int32)
    col_ids = col_start + jnp.arange(col_emb.shape[0], dtype=jnp.int32)
    diagonal = row_ids[:, None] == col_ids[None, :]
    return (jnp.where(diagonal, pref_rows[:, None], dist), diagonal)


def top_two(summed):
    first = jnp.max(summed, axis=1)
    hits = summed == first[:, None]
    repeats = jnp.sum(hits.astype(jnp.int32), axis=1)
    others = jnp.max(jnp.where(hits, -jnp.inf, summed), axis=1)
    second = jnp.where(repeats > 1, first, others)
    return (first, second)


def tiled(embedding, preference):
    rows_n = lax.axis_size("row")
    cols_n = lax.axis_size("col")
    row_idx = lax.axis_index("row")
    col_idx = lax.axis_index("col")
    mol = embedding.shape[2]
    width = embedding.shape[3]
    row_count = mol * cols_n
    col_count = mol * rows_n
    column_block = lax.all_gather(embedding, "row", axis=1, tiled=True).reshape(col_count, width)
    offset = row_idx * cols_n % rows_n
    root = row_idx * cols_n // rows_n
    own_slice = lax.dynamic_slice_in_dim(column_block, offset * mol, row_count, 0)
    row_block = broadcast(own_slice, "col", root)
    row_start = row_idx * row_count
    col_start = col_idx * col_count
    sim, diagonal = similarity(row_block, column_block, row_start, col_start, preference)
    resp = jnp.zeros_like(sim)
    avail = jnp.zeros_like(sim)
    for step in range(ITERS):
        summed = avail + sim
        local_first, local_second = top_two(summed)
        firsts, seconds = (
            lax.all_gather(local_first, "col", axis=0, tiled=True),
            lax.all_gather(local_second, "col", axis=0, tiled=True),
        )
        firsts = firsts.reshape(cols_n, row_count)
        seconds = seconds.reshape(cols_n, row_count)
        first = jnp.max(firsts, axis=0)
        at_top = firsts == first[None, :]
        repeats = jnp.sum(at_top.astype(jnp.int32), axis=0)
        others = jnp.max(jnp.where(at_top, -jnp.inf, firsts), axis=0)
        second = jnp.where(repeats > 1, first, jnp.maximum(jnp.max(seconds, axis=0), others))
        fresh = sim - jnp.where(summed == first[:, None], second[:, None], first[:, None])
        resp = DAMPING * resp + (1.0 - DAMPING) * fresh
        positive = jnp.where(diagonal, resp, jnp.maximum(resp, 0.0))
        colsum = lax.psum(jnp.sum(positive, axis=0), "row")
        renew = colsum[None, :] - positive
        renew = jnp.where(diagonal, renew, jnp.minimum(renew, 0.0))
        avail = DAMPING * avail + (1.0 - DAMPING) * renew
    return (resp, avail)


def solution(mesh):
    placed = (P("col", "row", None, None), P("row"))
    return jax.shard_map(
        local,
        mesh=mesh,
        in_specs=placed,
        out_specs=(P("row", "col"), P("row", "col")),
        check_vma=False,
    )
```

```python
import functools
import math

import jax
import jax.numpy as jnp
from jax import lax
from jax.experimental import pallas as pl
from jax.experimental.pallas import tpu as pltpu
from jax.sharding import PartitionSpec as P

ITERS = 2
DAMPING = 0.5
LOW = -1e30
LANES = 128
NT = (((1,), (1,)), ((), ()))
F32, BF16 = jnp.float32, jnp.bfloat16


def push(one, two, item):
    return jnp.maximum(one, item), jnp.maximum(two, jnp.minimum(one, item))


def merge(one, two, o, t):
    return jnp.maximum(one, o), jnp.maximum(jnp.minimum(one, o), jnp.maximum(two, t))


def fold(one, two, at=None):
    for shift in (4, 2, 1):
        o, t = pltpu.roll(one, shift, 0), pltpu.roll(two, shift, 0)
        if at is not None:
            a = pltpu.roll(at, shift, 0)
            at = jnp.where((o > one) | ((o == one) & (a < at)), a, at)
        one, two = merge(one, two, o, t)
    return one, two, at


def thirds(value):
    high = value.astype(BF16).astype(F32)
    rest = value - high
    mid = rest.astype(BF16).astype(F32)
    return high, mid, rest - mid


def squares(x_ref, q_ref, step):
    n, width = x_ref.shape
    ones = jnp.ones((2 * width, LANES), BF16)
    for s in range(0, n, step):
        x = x_ref[s:s + step, :].astype(F32)
        x = x * x
        high = x.astype(BF16)
        low = (x - high.astype(F32)).astype(BF16)
        q_ref[s:s + step, :] = jnp.dot(jnp.concatenate([high, low], 1), ones, preferred_element_type=F32)


def unpack(mesh_n, mol, owners, me, pieces, x_ref, pref_ref):
    rows_n, cols_n = mesh_n
    tails = [None, None]
    for i, (piece, masks) in enumerate(zip(pieces, owners)):
        for p, mask in enumerate(masks):
            owner = me ^ mask
            row, col = owner // cols_n, owner % cols_n
            x_ref[pl.ds(pl.multiple_of((col * rows_n + row) * mol, 16), mol), :] = piece[p * mol:(p + 1) * mol, :]
        if i < len(pieces) // 2 and masks[0] % cols_n // 2 < 2:
            flip = masks[0] // cols_n
            tail = piece[len(masks) * mol:len(masks) * mol + 8, :].astype(F32)
            tails[flip] = tail if tails[flip] is None else tails[flip] + tail
    for flip, tail in enumerate(tails):
        for far in range(rows_n // 2):
            pref_ref[pl.ds(2 * far + (me // cols_n % 2 ^ flip), 1), :] = tail[2 * far:2 * far + 1] + tail[2 * far + 1:2 * far + 2]


FIRST, GAIN, OWN, R1D, ONE, TWO, BASE, Z, R2D, AV1D, STAR, WZ = range(12)


def kernel(mesh_n, mol, owners, rows, cols, win, *refs, T=512, R=256, QS=256):
    pieces, refs = refs[:len(owners)], refs[len(owners):]
    resp_ref, avail_ref, x_ref, pref_ref, g_ref, c_ref, a_ref, q_ref, row_ref, k_ref, r_out, a_out, t_ref, out_sem = refs
    n, width = x_ref.shape
    rows_n, cols_n = mesh_n
    row_idx, col_idx = lax.axis_index("row"), lax.axis_index("col")
    unpack(mesh_n, mol, owners, row_idx * cols_n + col_idx, pieces, x_ref, pref_ref)
    squares(x_ref, q_ref, QS)
    sub8 = lax.broadcasted_iota(jnp.int32, (8, LANES), 0)
    lane8 = lax.broadcasted_iota(jnp.int32, (8, LANES), 1)
    gap = lane8 - sub8
    pref = jnp.concatenate([pref_ref[r:r + 1, 0:rows] for r in range(rows_n)], 1)
    blocks = n // LANES
    low8 = jnp.full((8, LANES), LOW, F32)
    for t in range(0, n, T):
        xt = x_ref[t:t + T, :] * BF16(2)
        K = T // LANES
        one, two, at = [low8] * K, [low8] * K, [jnp.zeros((8, LANES), jnp.int32)] * K
        dq = [jnp.zeros((8, LANES), F32)] * K
        for b in range(0, n, R):
            p = lax.dot_general(x_ref[b:b + R, :], xt, NT, preferred_element_type=F32)
            for r in range(0, R, 8):
                q = q_ref[b + r:b + r + 8, :]
                for l in range(K):
                    item = p[r:r + 8, l * LANES:(l + 1) * LANES]
                    lo = t + l * LANES
                    on = lo <= b + r < lo + LANES
                    if on:
                        mask = gap == b + r - lo
                        dq[l] = dq[l] + jnp.where(mask, item, 0.0)
                    item = item - q
                    if on:
                        item = jnp.where(mask, LOW, item)
                    g_ref[b + r:b + r + 8, lo:lo + LANES] = item
                    at[l] = jnp.where(item > one[l], b + r, at[l])
                    one[l], two[l] = push(one[l], two[l], item)
        for l in range(K):
            lanes = slice(t + l * LANES, t + (l + 1) * LANES)
            top, next_, a = fold(one[l], two[l], at[l] + sub8)
            own = jnp.broadcast_to(pref[:, lanes] + 0.5 * jnp.sum(dq[l], axis=0, keepdims=True), (8, LANES))
            first, second = push(top, next_, own)
            row_ref[STAR, :, lanes] = top
            row_ref[FIRST, :, lanes] = first
            row_ref[GAIN, :, lanes] = jnp.maximum(0.25 * (top - jnp.maximum(next_, own)), 0.0)
            row_ref[OWN, :, lanes] = own
            row_ref[R1D, :, lanes] = 0.5 * (own - jnp.where(own == first, second, first))
            k_ref[0, :, lanes] = a
            k_ref[1, :, lanes] = a - sub8
    H = -(-blocks // 16) * 16
    subL = lax.broadcasted_iota(jnp.int32, (LANES, LANES), 0)
    subH = lax.broadcasted_iota(jnp.int32, (H, LANES), 0)
    short, diag, tall, eyes = [[], [], []], [[], [], []], [], []
    eye = jnp.where(subL == lax.broadcasted_iota(jnp.int32, (LANES, LANES), 1), 1.0, 0.0).astype(BF16)
    for l in range(blocks):
        lanes = slice(l * LANES, (l + 1) * LANES)
        k = k_ref[0, 0:1, lanes]
        eyes.append(eye)
        for i, part in enumerate(thirds(0.5 * row_ref[R1D, 0:1, lanes])):
            diag[i].append(jnp.where(subH == l, part, 0.0).astype(BF16))
        tall.append(jnp.where(subL == k % LANES, 1.0, 0.0).astype(BF16))
        for i, part in enumerate(thirds(row_ref[GAIN, 0:1, lanes])):
            short[i].append(jnp.where(subH == k // LANES, part, 0.0).astype(BF16))
    tall, eyes = jnp.concatenate(tall, 1), jnp.concatenate(eyes, 1)
    short = jnp.concatenate([jnp.concatenate(s, 1) for s in short], 0)
    diag = jnp.concatenate([jnp.concatenate(s, 1) for s in diag], 0)
    s = lax.dot_general(short, tall, NT, preferred_element_type=F32)
    s = (s[0:H] + s[H:2 * H]) + s[2 * H:]
    side = lax.dot_general(jnp.concatenate([tall, eyes], 1), jnp.concatenate([short, diag], 1), NT, preferred_element_type=F32)
    side = (side[:, 0:H] + side[:, H:2 * H]) + side[:, 2 * H:]
    half = []
    for l in range(blocks):
        lanes = slice(l * LANES, (l + 1) * LANES)
        c = jnp.broadcast_to(side[:, l:l + 1], (LANES, LANES))
        c_ref[:, lanes] = c
        a_ref[:, lanes] = jnp.minimum(c, 0.0)
        av = s[l:l + 1, :]
        row_ref[AV1D, :, lanes] = jnp.broadcast_to(av, (8, LANES))
        half.append(av + 0.5 * row_ref[R1D, 0:1, lanes])
    half = jnp.concatenate(half + [jnp.zeros((H - blocks, LANES), F32)] * (H > blocks), 0)
    half = jnp.concatenate(thirds(half), 0).astype(BF16)
    got = jnp.dot(half, tall, preferred_element_type=F32)
    got = (got[0:H] + got[H:2 * H]) + got[2 * H:]
    for l in range(blocks):
        lanes = slice(l * LANES, (l + 1) * LANES)
        k = k_ref[0, 0:1, lanes]
        c = jnp.sum(jnp.where(subH == k // LANES, got[:, lanes], 0.0), axis=0, keepdims=True)
        row_ref[WZ, :, lanes] = jnp.broadcast_to(c, (8, LANES))
    for t in range(0, n, T):
        K = T // LANES
        lanes = [slice(t + l * LANES, t + (l + 1) * LANES) for l in range(K)]
        star = [k_ref[1, :, k] for k in lanes]
        def tops(j, tops):
            one, two = list(tops[:K]), list(tops[K:])
            base = pl.multiple_of(j * LANES, LANES)
            near = [s - base for s in star]
            for r in range(0, LANES, 8):
                a = a_ref[r:r + 8, pl.ds(base, LANES)]
                for l, k in enumerate(lanes):
                    u = jnp.where(near[l] == r, LOW, g_ref[pl.ds(pl.multiple_of(base + r, 8), 8), k] + a)
                    one[l], two[l] = push(one[l], two[l], u)
            return one + two
        ends = lax.fori_loop(0, blocks, tops, [low8] * (2 * K))
        for l, k in enumerate(lanes):
            row_ref[ONE, :, k], row_ref[TWO, :, k], _ = fold(ends[l], ends[K + l])
    for l in range(blocks):
        k = slice(l * LANES, (l + 1) * LANES)
        one, two = row_ref[ONE, :, k], row_ref[TWO, :, k]
        own, r1d, first, gain, av1d = (row_ref[i, :, k] for i in (OWN, R1D, FIRST, GAIN, AV1D))
        t = jnp.minimum(row_ref[WZ, :, k] - gain, 0.0)
        star = row_ref[STAR, :, k] + t
        own2 = own + av1d
        one, two = push(one, two, star)
        one, two = push(one, two, own2)
        z = (2 / 3) * (one - two)
        row_ref[ONE, :, k] = one
        row_ref[BASE, :, k] = (first + 2.0 * one) * (1 / 3)
        row_ref[Z, :, k] = z
        row_ref[R2D, :, k] = 0.5 * r1d + 0.5 * (own - jnp.where(own2 == one, two, one))
        row_ref[WZ, :, k] = (4 / 3) * gain + jnp.where(star == one, z, 0.0)
        row_ref[STAR, :, k] = t
    r0, c0 = row_idx * rows, col_idx * cols
    off = pl.multiple_of(r0 % LANES, 8)
    w0 = pl.multiple_of((r0 // LANES) * LANES, LANES)
    def block(j):
        st = pl.multiple_of(c0 + j * LANES, LANES)
        groups = LANES // 8
        at = [pl.ds(pl.multiple_of(st + 8 * r, 8), 8) for r in range(groups)]
        a = [a_ref[8 * r:8 * r + 8, pl.ds(st, LANES)] for r in range(groups)]
        r2d = (4 / 3) * row_ref[R2D, :, pl.ds(st, LANES)]
        acc = [jnp.where(gap == 8 * r, r2d, 0.0) for r in range(groups)]
        def resp2(r, k, star, row):
            g = g_ref[at[r], k]
            more = jnp.where(g + a[r] == row[0], row[2], 0.0)
            return (g - row[1]) + jnp.where(star == 8 * r, row[3], more)
        for l in range(blocks):
            k = slice(l * LANES, (l + 1) * LANES)
            star = k_ref[1, :, k] - st
            row = [row_ref[i, :, k] for i in (ONE, BASE, Z, WZ)]
            for r in range(groups):
                acc[r] = acc[r] + jnp.maximum(resp2(r, k, star, row), 0.0)
        cs = [0.375 * jnp.broadcast_to(jnp.sum(v, axis=1, keepdims=True), (8, LANES)) for v in acc]
        for l in range(0, win, LANES):
            k = pl.ds(pl.multiple_of(w0 + l, LANES), LANES)
            star = k_ref[1, :, k] - st
            row = [row_ref[i, :, k] for i in (ONE, BASE, Z, WZ)]
            rd, ad, ts = row_ref[R2D, :, k], row_ref[AV1D, :, k], row_ref[STAR, :, k]
            for r in range(groups):
                r2 = 0.75 * resp2(r, k, star, row)
                t = jnp.where(star == 8 * r, ts, a[r])
                a2 = 0.5 * t + jnp.minimum(cs[r] - 0.5 * jnp.maximum(r2, 0.0), 0.0)
                dg = gap == st + 8 * r - (w0 + l)
                r_out[8 * r:8 * r + 8, j * win + l:j * win + l + LANES] = jnp.where(dg, rd, r2)
                a_out[8 * r:8 * r + 8, j * win + l:j * win + l + LANES] = jnp.where(dg, 0.5 * ad + (cs[r] - 0.5 * rd), a2)
        lanes = slice(j * LANES, (j + 1) * LANES)
        for i, (tile, out_ref) in enumerate(((r_out, resp_ref), (a_out, avail_ref))):
            t_ref[i, :, lanes] = tile[:, j * win:(j + 1) * win].T
            copy = pltpu.make_async_copy(t_ref.at[i, pl.ds(off, rows), lanes], out_ref.at[:, lanes], out_sem.at[j, i])
            copy.start()
            copies.append(copy)
    copies = []
    for j in range(cols // LANES):
        block(j)
    for copy in copies:
        copy.wait()


def compute(pieces, mesh_n, mol, owners, rows, cols):
    n, width = mol * mesh_n[0] * mesh_n[1], pieces[0].shape[1]
    win = -(-(rows + LANES - math.gcd(rows, LANES)) // LANES) * LANES
    return pl.pallas_call(
        functools.partial(kernel, mesh_n, mol, owners, rows, cols, win),
        out_shape=[jax.ShapeDtypeStruct((rows, cols), F32)] * 2,
        in_specs=[pl.BlockSpec(memory_space=pltpu.VMEM)] * len(pieces),
        out_specs=[pl.BlockSpec(memory_space=pl.ANY)] * 2,
        scratch_shapes=[
            pltpu.VMEM((n, width), BF16),
            pltpu.VMEM((mesh_n[0], width), F32),
            pltpu.VMEM((n, n), F32),
            pltpu.VMEM((LANES, n), F32),
            pltpu.VMEM((LANES, n), F32),
            pltpu.VMEM((n, LANES), F32),
            pltpu.VMEM((12, 8, n), F32),
            pltpu.VMEM((2, 8, n), jnp.int32),
            pltpu.VMEM((LANES, cols // LANES * win), F32),
            pltpu.VMEM((LANES, cols // LANES * win), F32),
            pltpu.VMEM((2, win, cols), F32),
            pltpu.SemaphoreType.DMA((cols // LANES, 2)),
        ],
        compiler_params=pltpu.CompilerParams(vmem_limit_bytes=40 << 20),
    )(*pieces)


def pack_kernel(mol, embedding_ref, preference_ref, out_ref, e_ref, p_ref, sems):
    copies = [
        pltpu.make_async_copy(preference_ref, p_ref, sems.at[0]),
        pltpu.make_async_copy(embedding_ref, e_ref, sems.at[1]),
    ]
    for copy in copies:
        copy.start()
    for copy in copies:
        copy.wait()
    out_ref[0:mol, :] = e_ref[...]
    values = p_ref[...]
    high, mid, low = thirds(values)
    odd = lax.axis_index("col") // 2 % 2 == 1
    fill = jnp.zeros((1, out_ref.shape[1] - values.shape[1]), F32)
    one, two = (jnp.concatenate([part, fill], 1) for part in (jnp.where(odd, low, high), jnp.where(odd, 0.0, mid)))
    at = lax.broadcasted_iota(jnp.int32, (8, out_ref.shape[1]), 0) - lax.axis_index("row") // 2 * 2
    out_ref[mol:mol + 8, :] = jnp.where(at == 0, one, jnp.where(at == 1, two, 0.0)).astype(BF16)


def pack(embedding, preference):
    mol, width = embedding.shape
    return pl.pallas_call(
        functools.partial(pack_kernel, mol),
        out_shape=pltpu.VMEM((mol + 8, width), BF16),
        in_specs=[pl.BlockSpec(memory_space=pltpu.HBM)] * 2,
        out_specs=pl.BlockSpec(memory_space=pltpu.VMEM),
        scratch_shapes=[pltpu.VMEM((mol, width), BF16), pltpu.VMEM(preference.shape, F32), pltpu.SemaphoreType.DMA((2,))],
        compiler_params=pltpu.CompilerParams(vmem_limit_bytes=60 << 20),
    )(embedding, preference)


def fits(rows_n, cols_n, mol, width):
    n = mol * rows_n * cols_n
    two = rows_n in (2, 4, 8) and cols_n >= 4 and not cols_n & (cols_n - 1)
    return (two and 4 * n * n <= 16 << 20 and n % 512 == 0 and mol * rows_n % LANES == 0 and mol % 16 == 0
            and mol * cols_n <= width and width % LANES == 0)


def stages(rows_n, cols_n):
    far = [m * 2 * cols_n + 1 for m in range(1,rows_n//2)]
    near = [m * 2 + 1 for m in range(1,cols_n)]
    return far, near


def swap(block, mask):
    size = lax.axis_size("row") * lax.axis_size("col")
    return lax.ppermute(block, ("row", "col"), [(i, i ^ mask) for i in range(size)])


def replicated(embedding, preference):
    rows_n, cols_n = lax.axis_size("row"), lax.axis_size("col")
    mol, width = embedding.shape[2:]
    rows, cols = mol * cols_n, mol * rows_n
    held = pack(embedding.reshape(mol, width), preference.reshape(1, rows))
    far, near = stages(rows_n, cols_n)
    line = [held] + [swap(held, m) for m in far]
    line = jnp.concatenate([h[:mol] for h in line] + [sum(h[mol:] for h in line)], 0)
    pieces = [line] + [swap(line, m) for m in near]
    owners = [[n ^ f for f in [0] + far] for n in [0] + near]
    pieces = pieces + [swap(piece, 1) for piece in pieces]
    owners = owners + [[m ^ 1 for m in masks] for masks in owners]
    return tuple(compute(pieces, (rows_n, cols_n), mol, owners, rows, cols))


def local(embedding, preference):
    if fits(lax.axis_size("row"), lax.axis_size("col"), *embedding.shape[2:]):
        return replicated(embedding, preference)
    return tiled(embedding, preference)


def broadcast(block, axis, source):
    block = jnp.where(lax.axis_index(axis) == source, block, jnp.zeros_like(block))
    return lax.psum(block, axis)


def similarity(row_emb, col_emb, row_start, col_start, pref_rows):
    cross = lax.dot_general(
        row_emb, col_emb, (((1,), (1,)), ((), ())), preferred_element_type=jnp.float32
    )
    row_vals = row_emb.astype(jnp.float32)
    col_vals = col_emb.astype(jnp.float32)
    row_sq = jnp.sum(row_vals * row_vals, axis=1)
    col_sq = jnp.sum(col_vals * col_vals, axis=1)
    dist = 2.0 * cross - row_sq[:, None] - col_sq[None, :]
    row_ids = row_start + jnp.arange(row_emb.shape[0], dtype=jnp.int32)
    col_ids = col_start + jnp.arange(col_emb.shape[0], dtype=jnp.int32)
    diagonal = row_ids[:, None] == col_ids[None, :]
    return (jnp.where(diagonal, pref_rows[:, None], dist), diagonal)


def top_two(summed):
    first = jnp.max(summed, axis=1)
    hits = summed == first[:, None]
    repeats = jnp.sum(hits.astype(jnp.int32), axis=1)
    others = jnp.max(jnp.where(hits, -jnp.inf, summed), axis=1)
    second = jnp.where(repeats > 1, first, others)
    return (first, second)


def tiled(embedding, preference):
    rows_n = lax.axis_size("row")
    cols_n = lax.axis_size("col")
    row_idx = lax.axis_index("row")
    col_idx = lax.axis_index("col")
    mol = embedding.shape[2]
    width = embedding.shape[3]
    row_count = mol * cols_n
    col_count = mol * rows_n
    column_block = lax.all_gather(embedding, "row", axis=1, tiled=True).reshape(col_count, width)
    offset = row_idx * cols_n % rows_n
    root = row_idx * cols_n // rows_n
    own_slice = lax.dynamic_slice_in_dim(column_block, offset * mol, row_count, 0)
    row_block = broadcast(own_slice, "col", root)
    row_start = row_idx * row_count
    col_start = col_idx * col_count
    sim, diagonal = similarity(row_block, column_block, row_start, col_start, preference)
    resp = jnp.zeros_like(sim)
    avail = jnp.zeros_like(sim)
    for step in range(ITERS):
        summed = avail + sim
        local_first, local_second = top_two(summed)
        firsts, seconds = (
            lax.all_gather(local_first, "col", axis=0, tiled=True),
            lax.all_gather(local_second, "col", axis=0, tiled=True),
        )
        firsts = firsts.reshape(cols_n, row_count)
        seconds = seconds.reshape(cols_n, row_count)
        first = jnp.max(firsts, axis=0)
        at_top = firsts == first[None, :]
        repeats = jnp.sum(at_top.astype(jnp.int32), axis=0)
        others = jnp.max(jnp.where(at_top, -jnp.inf, firsts), axis=0)
        second = jnp.where(repeats > 1, first, jnp.maximum(jnp.max(seconds, axis=0), others))
        fresh = sim - jnp.where(summed == first[:, None], second[:, None], first[:, None])
        resp = DAMPING * resp + (1.0 - DAMPING) * fresh
        positive = jnp.where(diagonal, resp, jnp.maximum(resp, 0.0))
        colsum = lax.psum(jnp.sum(positive, axis=0), "row")
        renew = colsum[None, :] - positive
        renew = jnp.where(diagonal, renew, jnp.minimum(renew, 0.0))
        avail = DAMPING * avail + (1.0 - DAMPING) * renew
    return (resp, avail)


def solution(mesh):
    placed = (P("col", "row", None, None), P("row"))
    return jax.shard_map(
        local,
        mesh=mesh,
        in_specs=placed,
        out_specs=(P("row", "col"), P("row", "col")),
        check_vma=False,
    )
```

```python
import functools
import math

import jax
import jax.numpy as jnp
from jax import lax
from jax.experimental import pallas as pl
from jax.experimental.pallas import tpu as pltpu
from jax.sharding import PartitionSpec as P

ITERS = 2
DAMPING = 0.5
LOW = -1e30
LANES = 128
NT = (((1,), (1,)), ((), ()))
F32, BF16 = jnp.float32, jnp.bfloat16


def push(one, two, item):
    return jnp.maximum(one, item), jnp.maximum(two, jnp.minimum(one, item))


def merge(one, two, o, t):
    return jnp.maximum(one, o), jnp.maximum(jnp.minimum(one, o), jnp.maximum(two, t))


def fold(one, two, at=None):
    for shift in (4, 2, 1):
        o, t = pltpu.roll(one, shift, 0), pltpu.roll(two, shift, 0)
        if at is not None:
            a = pltpu.roll(at, shift, 0)
            at = jnp.where((o > one) | ((o == one) & (a < at)), a, at)
        one, two = merge(one, two, o, t)
    return one, two, at


def thirds(value):
    high = value.astype(BF16).astype(F32)
    rest = value - high
    mid = rest.astype(BF16).astype(F32)
    return high, mid, rest - mid


def squares(x):
    ones = jnp.ones((2 * x.shape[1], LANES), BF16)
    x = x.astype(F32)
    x = x * x
    high = x.astype(BF16)
    low = (x - high.astype(F32)).astype(BF16)
    return jnp.dot(jnp.concatenate([high, low], 1), ones, preferred_element_type=F32)


def unpack(mesh_n, mol, owners, me, pieces, early, early_ref, x_ref, q_ref, pref_ref):
    rows_n, cols_n = mesh_n
    tails = [None, None]
    for i, (piece, masks) in enumerate(zip(pieces, owners)):
        if i not in early:
            q = squares(piece[0:len(masks) * mol, :])
        for p, mask in enumerate(masks):
            owner = me ^ mask
            row, col = owner // cols_n, owner % cols_n
            at = pl.ds(pl.multiple_of((col * rows_n + row) * mol, 16), mol)
            x_ref[at, :] = piece[p * mol:(p + 1) * mol, :]
            if i in early:
                start = (early.index(i) * len(masks) + p) * mol
                q_ref[at, :] = early_ref[start:start + mol, :]
            else:
                q_ref[at, :] = q[p * mol:(p + 1) * mol, :]
        if i < len(pieces) // 2 and masks[0] % cols_n // 2 < 2:
            flip = masks[0] // cols_n
            tail = piece[len(masks) * mol:len(masks) * mol + 8, :].astype(F32)
            tails[flip] = tail if tails[flip] is None else tails[flip] + tail
    for flip, tail in enumerate(tails):
        for far in range(rows_n // 2):
            pref_ref[pl.ds(2 * far + (me // cols_n % 2 ^ flip), 1), :] = tail[2 * far:2 * far + 1] + tail[2 * far + 1:2 * far + 2]


FIRST, GAIN, OWN, R1D, ONE, TWO, BASE, Z, R2D, AV1D, STAR, WZ = range(12)


def kernel(mesh_n, mol, owners, early, rows, cols, win, *refs, T=512, R=256):
    early_ref, pieces, refs = refs[0], refs[1:len(owners) + 1], refs[len(owners) + 1:]
    resp_ref, avail_ref, x_ref, pref_ref, g_ref, c_ref, a_ref, q_ref, row_ref, k_ref, r_out, a_out, t_ref, out_sem = refs
    n, width = x_ref.shape
    rows_n, cols_n = mesh_n
    row_idx, col_idx = lax.axis_index("row"), lax.axis_index("col")
    unpack(mesh_n, mol, owners, row_idx * cols_n + col_idx, pieces, early, early_ref, x_ref, q_ref, pref_ref)
    sub8 = lax.broadcasted_iota(jnp.int32, (8, LANES), 0)
    lane8 = lax.broadcasted_iota(jnp.int32, (8, LANES), 1)
    gap = lane8 - sub8
    pref = jnp.concatenate([pref_ref[r:r + 1, 0:rows] for r in range(rows_n)], 1)
    blocks = n // LANES
    low8 = jnp.full((8, LANES), LOW, F32)
    for t in range(0, n, T):
        xt = x_ref[t:t + T, :] * BF16(2)
        K = T // LANES
        one, two, at = [low8] * K, [low8] * K, [jnp.zeros((8, LANES), jnp.int32)] * K
        dq = [jnp.zeros((8, LANES), F32)] * K
        for b in range(0, n, R):
            p = lax.dot_general(x_ref[b:b + R, :], xt, NT, preferred_element_type=F32)
            for r in range(0, R, 8):
                q = q_ref[b + r:b + r + 8, :]
                for l in range(K):
                    item = p[r:r + 8, l * LANES:(l + 1) * LANES]
                    lo = t + l * LANES
                    on = lo <= b + r < lo + LANES
                    if on:
                        mask = gap == b + r - lo
                        dq[l] = dq[l] + jnp.where(mask, item, 0.0)
                    item = item - q
                    if on:
                        item = jnp.where(mask, LOW, item)
                    g_ref[b + r:b + r + 8, lo:lo + LANES] = item
                    at[l] = jnp.where(item > one[l], b + r, at[l])
                    one[l], two[l] = push(one[l], two[l], item)
        for l in range(K):
            lanes = slice(t + l * LANES, t + (l + 1) * LANES)
            top, next_, a = fold(one[l], two[l], at[l] + sub8)
            own = jnp.broadcast_to(pref[:, lanes] + 0.5 * jnp.sum(dq[l], axis=0, keepdims=True), (8, LANES))
            first, second = push(top, next_, own)
            row_ref[STAR, :, lanes] = top
            row_ref[FIRST, :, lanes] = first
            row_ref[GAIN, :, lanes] = jnp.maximum(0.25 * (top - jnp.maximum(next_, own)), 0.0)
            row_ref[OWN, :, lanes] = own
            row_ref[R1D, :, lanes] = 0.5 * (own - jnp.where(own == first, second, first))
            k_ref[0, :, lanes] = a
            k_ref[1, :, lanes] = a - sub8
    H = -(-blocks // 16) * 16
    subL = lax.broadcasted_iota(jnp.int32, (LANES, LANES), 0)
    subH = lax.broadcasted_iota(jnp.int32, (H, LANES), 0)
    short, diag, tall, eyes = [[], [], []], [[], [], []], [], []
    eye = jnp.where(subL == lax.broadcasted_iota(jnp.int32, (LANES, LANES), 1), 1.0, 0.0).astype(BF16)
    for l in range(blocks):
        lanes = slice(l * LANES, (l + 1) * LANES)
        k = k_ref[0, 0:1, lanes]
        eyes.append(eye)
        for i, part in enumerate(thirds(0.5 * row_ref[R1D, 0:1, lanes])):
            diag[i].append(jnp.where(subH == l, part, 0.0).astype(BF16))
        tall.append(jnp.where(subL == k % LANES, 1.0, 0.0).astype(BF16))
        for i, part in enumerate(thirds(row_ref[GAIN, 0:1, lanes])):
            short[i].append(jnp.where(subH == k // LANES, part, 0.0).astype(BF16))
    tall, eyes = jnp.concatenate(tall, 1), jnp.concatenate(eyes, 1)
    short = jnp.concatenate([jnp.concatenate(s, 1) for s in short], 0)
    diag = jnp.concatenate([jnp.concatenate(s, 1) for s in diag], 0)
    s = lax.dot_general(short, tall, NT, preferred_element_type=F32)
    s = (s[0:H] + s[H:2 * H]) + s[2 * H:]
    side = lax.dot_general(jnp.concatenate([tall, eyes], 1), jnp.concatenate([short, diag], 1), NT, preferred_element_type=F32)
    side = (side[:, 0:H] + side[:, H:2 * H]) + side[:, 2 * H:]
    half = []
    for l in range(blocks):
        lanes = slice(l * LANES, (l + 1) * LANES)
        c = jnp.broadcast_to(side[:, l:l + 1], (LANES, LANES))
        c_ref[:, lanes] = c
        a_ref[:, lanes] = jnp.minimum(c, 0.0)
        av = s[l:l + 1, :]
        row_ref[AV1D, :, lanes] = jnp.broadcast_to(av, (8, LANES))
        half.append(av + 0.5 * row_ref[R1D, 0:1, lanes])
    half = jnp.concatenate(half + [jnp.zeros((H - blocks, LANES), F32)] * (H > blocks), 0)
    half = jnp.concatenate(thirds(half), 0).astype(BF16)
    got = jnp.dot(half, tall, preferred_element_type=F32)
    got = (got[0:H] + got[H:2 * H]) + got[2 * H:]
    for l in range(blocks):
        lanes = slice(l * LANES, (l + 1) * LANES)
        k = k_ref[0, 0:1, lanes]
        c = jnp.sum(jnp.where(subH == k // LANES, got[:, lanes], 0.0), axis=0, keepdims=True)
        row_ref[WZ, :, lanes] = jnp.broadcast_to(c, (8, LANES))
    for t in range(0, n, T):
        K = T // LANES
        lanes = [slice(t + l * LANES, t + (l + 1) * LANES) for l in range(K)]
        star = [k_ref[1, :, k] for k in lanes]
        def tops(j, tops):
            one, two = list(tops[:K]), list(tops[K:])
            base = pl.multiple_of(j * LANES, LANES)
            near = [s - base for s in star]
            for r in range(0, LANES, 8):
                a = a_ref[r:r + 8, pl.ds(base, LANES)]
                for l, k in enumerate(lanes):
                    u = jnp.where(near[l] == r, LOW, g_ref[pl.ds(pl.multiple_of(base + r, 8), 8), k] + a)
                    one[l], two[l] = push(one[l], two[l], u)
            return one + two
        ends = lax.fori_loop(0, blocks, tops, [low8] * (2 * K))
        for l, k in enumerate(lanes):
            row_ref[ONE, :, k], row_ref[TWO, :, k], _ = fold(ends[l], ends[K + l])
    for l in range(blocks):
        k = slice(l * LANES, (l + 1) * LANES)
        one, two = row_ref[ONE, :, k], row_ref[TWO, :, k]
        own, r1d, first, gain, av1d = (row_ref[i, :, k] for i in (OWN, R1D, FIRST, GAIN, AV1D))
        t = jnp.minimum(row_ref[WZ, :, k] - gain, 0.0)
        star = row_ref[STAR, :, k] + t
        own2 = own + av1d
        one, two = push(one, two, star)
        one, two = push(one, two, own2)
        z = (2 / 3) * (one - two)
        row_ref[ONE, :, k] = one
        row_ref[BASE, :, k] = (first + 2.0 * one) * (1 / 3)
        row_ref[Z, :, k] = z
        row_ref[R2D, :, k] = 0.5 * r1d + 0.5 * (own - jnp.where(own2 == one, two, one))
        row_ref[WZ, :, k] = (4 / 3) * gain + jnp.where(star == one, z, 0.0)
        row_ref[STAR, :, k] = t
    r0, c0 = row_idx * rows, col_idx * cols
    off = pl.multiple_of(r0 % LANES, 8)
    w0 = pl.multiple_of((r0 // LANES) * LANES, LANES)
    def block(j):
        st = pl.multiple_of(c0 + j * LANES, LANES)
        groups = LANES // 8
        at = [pl.ds(pl.multiple_of(st + 8 * r, 8), 8) for r in range(groups)]
        a = [a_ref[8 * r:8 * r + 8, pl.ds(st, LANES)] for r in range(groups)]
        r2d = (4 / 3) * row_ref[R2D, :, pl.ds(st, LANES)]
        acc = [jnp.where(gap == 8 * r, r2d, 0.0) for r in range(groups)]
        def resp2(r, k, star, row):
            g = g_ref[at[r], k]
            more = jnp.where(g + a[r] == row[0], row[2], 0.0)
            return (g - row[1]) + jnp.where(star == 8 * r, row[3], more)
        for l in range(blocks):
            k = slice(l * LANES, (l + 1) * LANES)
            star = k_ref[1, :, k] - st
            row = [row_ref[i, :, k] for i in (ONE, BASE, Z, WZ)]
            for r in range(groups):
                acc[r] = acc[r] + jnp.maximum(resp2(r, k, star, row), 0.0)
        cs = [0.375 * jnp.broadcast_to(jnp.sum(v, axis=1, keepdims=True), (8, LANES)) for v in acc]
        for l in range(0, win, LANES):
            k = pl.ds(pl.multiple_of(w0 + l, LANES), LANES)
            star = k_ref[1, :, k] - st
            row = [row_ref[i, :, k] for i in (ONE, BASE, Z, WZ)]
            rd, ad, ts = row_ref[R2D, :, k], row_ref[AV1D, :, k], row_ref[STAR, :, k]
            for r in range(groups):
                r2 = 0.75 * resp2(r, k, star, row)
                t = jnp.where(star == 8 * r, ts, a[r])
                a2 = 0.5 * t + jnp.minimum(cs[r] - 0.5 * jnp.maximum(r2, 0.0), 0.0)
                dg = gap == st + 8 * r - (w0 + l)
                r_out[8 * r:8 * r + 8, j * win + l:j * win + l + LANES] = jnp.where(dg, rd, r2)
                a_out[8 * r:8 * r + 8, j * win + l:j * win + l + LANES] = jnp.where(dg, 0.5 * ad + (cs[r] - 0.5 * rd), a2)
        lanes = slice(j * LANES, (j + 1) * LANES)
        for i, (tile, out_ref) in enumerate(((r_out, resp_ref), (a_out, avail_ref))):
            t_ref[i, :, lanes] = tile[:, j * win:(j + 1) * win].T
            copy = pltpu.make_async_copy(t_ref.at[i, pl.ds(off, rows), lanes], out_ref.at[:, lanes], out_sem.at[j, i])
            copy.start()
            copies.append(copy)
    copies = []
    for j in range(cols // LANES):
        block(j)
    for copy in copies:
        copy.wait()


def squares_kernel(count, *refs):
    for i, piece in enumerate(refs[:-1]):
        refs[-1][i * count:(i + 1) * count, :] = squares(piece[0:count, :])


def compute(pieces, mesh_n, mol, owners, early, rows, cols):
    n, width = mol * mesh_n[0] * mesh_n[1], pieces[0].shape[1]
    win = -(-(rows + LANES - math.gcd(rows, LANES)) // LANES) * LANES
    count = len(owners[0]) * mol
    sums = pl.pallas_call(
        functools.partial(squares_kernel, count),
        out_shape=jax.ShapeDtypeStruct((len(early) * count, LANES), F32),
        in_specs=[pl.BlockSpec(memory_space=pltpu.VMEM)] * len(early),
        out_specs=pl.BlockSpec(memory_space=pltpu.VMEM),
        cost_estimate=pl.CostEstimate(flops=len(early) * count * 4 * width * LANES, bytes_accessed=4 << 20, transcendentals=0),
        compiler_params=pltpu.CompilerParams(vmem_limit_bytes=40 << 20),
    )(*[pieces[i] for i in early])
    return pl.pallas_call(
        functools.partial(kernel, mesh_n, mol, owners, early, rows, cols, win),
        out_shape=[jax.ShapeDtypeStruct((rows, cols), F32)] * 2,
        in_specs=[pl.BlockSpec(memory_space=pltpu.VMEM)] * (len(pieces) + 1),
        out_specs=[pl.BlockSpec(memory_space=pl.ANY)] * 2,
        scratch_shapes=[
            pltpu.VMEM((n, width), BF16),
            pltpu.VMEM((mesh_n[0], width), F32),
            pltpu.VMEM((n, n), F32),
            pltpu.VMEM((LANES, n), F32),
            pltpu.VMEM((LANES, n), F32),
            pltpu.VMEM((n, LANES), F32),
            pltpu.VMEM((12, 8, n), F32),
            pltpu.VMEM((2, 8, n), jnp.int32),
            pltpu.VMEM((LANES, cols // LANES * win), F32),
            pltpu.VMEM((LANES, cols // LANES * win), F32),
            pltpu.VMEM((2, win, cols), F32),
            pltpu.SemaphoreType.DMA((cols // LANES, 2)),
        ],
        compiler_params=pltpu.CompilerParams(vmem_limit_bytes=40 << 20),
    )(sums, *pieces)


def pack_kernel(mol, embedding_ref, preference_ref, out_ref, e_ref, p_ref, sems):
    copies = [
        pltpu.make_async_copy(preference_ref, p_ref, sems.at[0]),
        pltpu.make_async_copy(embedding_ref, e_ref, sems.at[1]),
    ]
    for copy in copies:
        copy.start()
    for copy in copies:
        copy.wait()
    out_ref[0:mol, :] = e_ref[...]
    values = p_ref[...]
    high, mid, low = thirds(values)
    odd = lax.axis_index("col") // 2 % 2 == 1
    fill = jnp.zeros((1, out_ref.shape[1] - values.shape[1]), F32)
    one, two = (jnp.concatenate([part, fill], 1) for part in (jnp.where(odd, low, high), jnp.where(odd, 0.0, mid)))
    at = lax.broadcasted_iota(jnp.int32, (8, out_ref.shape[1]), 0) - lax.axis_index("row") // 2 * 2
    out_ref[mol:mol + 8, :] = jnp.where(at == 0, one, jnp.where(at == 1, two, 0.0)).astype(BF16)


def pack(embedding, preference):
    mol, width = embedding.shape
    return pl.pallas_call(
        functools.partial(pack_kernel, mol),
        out_shape=pltpu.VMEM((mol + 8, width), BF16),
        in_specs=[pl.BlockSpec(memory_space=pltpu.HBM)] * 2,
        out_specs=pl.BlockSpec(memory_space=pltpu.VMEM),
        scratch_shapes=[pltpu.VMEM((mol, width), BF16), pltpu.VMEM(preference.shape, F32), pltpu.SemaphoreType.DMA((2,))],
        compiler_params=pltpu.CompilerParams(vmem_limit_bytes=60 << 20),
    )(embedding, preference)


def fits(rows_n, cols_n, mol, width):
    n = mol * rows_n * cols_n
    two = rows_n in (2, 4, 8) and cols_n >= 4 and not cols_n & (cols_n - 1)
    return (two and 4 * n * n <= 16 << 20 and n % 512 == 0 and mol * rows_n % LANES == 0 and mol % 16 == 0
            and mol * cols_n <= width and width % LANES == 0)


def stages(rows_n, cols_n):
    far = [m * 2 * cols_n + 1 for m in range(1,rows_n//2)]
    near = [m * 2 + 1 for m in range(1,cols_n)]
    return far, near


def swap(block, mask):
    size = lax.axis_size("row") * lax.axis_size("col")
    return lax.ppermute(block, ("row", "col"), [(i, i ^ mask) for i in range(size)])


def replicated(embedding, preference):
    rows_n, cols_n = lax.axis_size("row"), lax.axis_size("col")
    mol, width = embedding.shape[2:]
    rows, cols = mol * cols_n, mol * rows_n
    held = pack(embedding.reshape(mol, width), preference.reshape(1, rows))
    far, near = stages(rows_n, cols_n)
    line = [held] + [swap(held, m) for m in far]
    line = jnp.concatenate([h[:mol] for h in line] + [sum(h[mol:] for h in line)], 0)
    pieces = [line] + [swap(line, m) for m in near]
    owners = [[n ^ f for f in [0] + far] for n in [0] + near]
    pieces = pieces + [swap(piece, 1) for piece in pieces]
    owners = owners + [[m ^ 1 for m in masks] for masks in owners]
    early = (*range(len(near) + 2), 2 * len(near) + 1)
    return tuple(compute(pieces, (rows_n, cols_n), mol, owners, early, rows, cols))


def local(embedding, preference):
    if fits(lax.axis_size("row"), lax.axis_size("col"), *embedding.shape[2:]):
        return replicated(embedding, preference)
    return tiled(embedding, preference)


def broadcast(block, axis, source):
    block = jnp.where(lax.axis_index(axis) == source, block, jnp.zeros_like(block))
    return lax.psum(block, axis)


def similarity(row_emb, col_emb, row_start, col_start, pref_rows):
    cross = lax.dot_general(
        row_emb, col_emb, (((1,), (1,)), ((), ())), preferred_element_type=jnp.float32
    )
    row_vals = row_emb.astype(jnp.float32)
    col_vals = col_emb.astype(jnp.float32)
    row_sq = jnp.sum(row_vals * row_vals, axis=1)
    col_sq = jnp.sum(col_vals * col_vals, axis=1)
    dist = 2.0 * cross - row_sq[:, None] - col_sq[None, :]
    row_ids = row_start + jnp.arange(row_emb.shape[0], dtype=jnp.int32)
    col_ids = col_start + jnp.arange(col_emb.shape[0], dtype=jnp.int32)
    diagonal = row_ids[:, None] == col_ids[None, :]
    return (jnp.where(diagonal, pref_rows[:, None], dist), diagonal)


def top_two(summed):
    first = jnp.max(summed, axis=1)
    hits = summed == first[:, None]
    repeats = jnp.sum(hits.astype(jnp.int32), axis=1)
    others = jnp.max(jnp.where(hits, -jnp.inf, summed), axis=1)
    second = jnp.where(repeats > 1, first, others)
    return (first, second)


def tiled(embedding, preference):
    rows_n = lax.axis_size("row")
    cols_n = lax.axis_size("col")
    row_idx = lax.axis_index("row")
    col_idx = lax.axis_index("col")
    mol = embedding.shape[2]
    width = embedding.shape[3]
    row_count = mol * cols_n
    col_count = mol * rows_n
    column_block = lax.all_gather(embedding, "row", axis=1, tiled=True).reshape(col_count, width)
    offset = row_idx * cols_n % rows_n
    root = row_idx * cols_n // rows_n
    own_slice = lax.dynamic_slice_in_dim(column_block, offset * mol, row_count, 0)
    row_block = broadcast(own_slice, "col", root)
    row_start = row_idx * row_count
    col_start = col_idx * col_count
    sim, diagonal = similarity(row_block, column_block, row_start, col_start, preference)
    resp = jnp.zeros_like(sim)
    avail = jnp.zeros_like(sim)
    for step in range(ITERS):
        summed = avail + sim
        local_first, local_second = top_two(summed)
        firsts, seconds = (
            lax.all_gather(local_first, "col", axis=0, tiled=True),
            lax.all_gather(local_second, "col", axis=0, tiled=True),
        )
        firsts = firsts.reshape(cols_n, row_count)
        seconds = seconds.reshape(cols_n, row_count)
        first = jnp.max(firsts, axis=0)
        at_top = firsts == first[None, :]
        repeats = jnp.sum(at_top.astype(jnp.int32), axis=0)
        others = jnp.max(jnp.where(at_top, -jnp.inf, firsts), axis=0)
        second = jnp.where(repeats > 1, first, jnp.maximum(jnp.max(seconds, axis=0), others))
        fresh = sim - jnp.where(summed == first[:, None], second[:, None], first[:, None])
        resp = DAMPING * resp + (1.0 - DAMPING) * fresh
        positive = jnp.where(diagonal, resp, jnp.maximum(resp, 0.0))
        colsum = lax.psum(jnp.sum(positive, axis=0), "row")
        renew = colsum[None, :] - positive
        renew = jnp.where(diagonal, renew, jnp.minimum(renew, 0.0))
        avail = DAMPING * avail + (1.0 - DAMPING) * renew
    return (resp, avail)


def solution(mesh):
    placed = (P("col", "row", None, None), P("row"))
    return jax.shard_map(
        local,
        mesh=mesh,
        in_specs=placed,
        out_specs=(P("row", "col"), P("row", "col")),
        check_vma=False,
    )
```

```python
import functools
import math

import jax
import jax.numpy as jnp
from jax import lax
from jax.experimental import pallas as pl
from jax.experimental.pallas import tpu as pltpu
from jax.sharding import PartitionSpec as P

ITERS = 2
DAMPING = 0.5
LOW = -1e30
LANES = 128
NT = (((1,), (1,)), ((), ()))
F32, BF16 = jnp.float32, jnp.bfloat16


def push(one, two, item):
    return jnp.maximum(one, item), jnp.maximum(two, jnp.minimum(one, item))


def merge(one, two, o, t):
    return jnp.maximum(one, o), jnp.maximum(jnp.minimum(one, o), jnp.maximum(two, t))


def fold(one, two, at=None):
    for shift in (4, 2, 1):
        o, t = pltpu.roll(one, shift, 0), pltpu.roll(two, shift, 0)
        if at is not None:
            a = pltpu.roll(at, shift, 0)
            at = jnp.where((o > one) | ((o == one) & (a < at)), a, at)
        one, two = merge(one, two, o, t)
    return one, two, at


def thirds(value):
    high = value.astype(BF16).astype(F32)
    rest = value - high
    mid = rest.astype(BF16).astype(F32)
    return high, mid, rest - mid


def squares(x):
    ones = jnp.ones((2 * x.shape[1], LANES), BF16)
    x = x.astype(F32)
    x = x * x
    high = x.astype(BF16)
    low = (x - high.astype(F32)).astype(BF16)
    return jnp.dot(jnp.concatenate([high, low], 1), ones, preferred_element_type=F32)


def place(mesh_n, mol, me, piece, masks, x_ref, q_ref):
    rows_n, cols_n = mesh_n
    q = squares(piece[0:len(masks) * mol, :])
    for p, mask in enumerate(masks):
        owner = me ^ mask
        row, col = owner // cols_n, owner % cols_n
        at = pl.ds(pl.multiple_of((col * rows_n + row) * mol, 16), mol)
        x_ref[at, :] = piece[p * mol:(p + 1) * mol, :]
        q_ref[at, :] = q[p * mol:(p + 1) * mol, :]


def unpack(mesh_n, mol, owners, me, pieces, early, x_ref, q_ref, pref_ref):
    rows_n, cols_n = mesh_n
    tails = [None, None]
    for i, (piece, masks) in enumerate(zip(pieces, owners)):
        if i not in early:
            place(mesh_n, mol, me, piece, masks, x_ref, q_ref)
        if i < len(pieces) // 2 and masks[0] % cols_n // 2 < 2:
            flip = masks[0] // cols_n
            tail = piece[len(masks) * mol:len(masks) * mol + 8, :].astype(F32)
            tails[flip] = tail if tails[flip] is None else tails[flip] + tail
    for flip, tail in enumerate(tails):
        for far in range(rows_n // 2):
            pref_ref[pl.ds(2 * far + (me // cols_n % 2 ^ flip), 1), :] = tail[2 * far:2 * far + 1] + tail[2 * far + 1:2 * far + 2]


FIRST, GAIN, OWN, R1D, ONE, TWO, BASE, Z, R2D, AV1D, STAR, WZ = range(12)


def kernel(mesh_n, mol, owners, early, rows, cols, win, *refs, T=512, R=256):
    pieces, refs = refs[2:len(owners) + 2], refs[len(owners) + 2:]
    resp_ref, avail_ref, x_ref, q_ref, pref_ref, g_ref, c_ref, a_ref, row_ref, k_ref, r_out, a_out, t_ref, out_sem = refs
    n, width = x_ref.shape
    rows_n, cols_n = mesh_n
    row_idx, col_idx = lax.axis_index("row"), lax.axis_index("col")
    unpack(mesh_n, mol, owners, row_idx * cols_n + col_idx, pieces, early, x_ref, q_ref, pref_ref)
    sub8 = lax.broadcasted_iota(jnp.int32, (8, LANES), 0)
    lane8 = lax.broadcasted_iota(jnp.int32, (8, LANES), 1)
    gap = lane8 - sub8
    pref = jnp.concatenate([pref_ref[r:r + 1, 0:rows] for r in range(rows_n)], 1)
    blocks = n // LANES
    low8 = jnp.full((8, LANES), LOW, F32)
    for t in range(0, n, T):
        xt = x_ref[t:t + T, :] * BF16(2)
        K = T // LANES
        one, two, at = [low8] * K, [low8] * K, [jnp.zeros((8, LANES), jnp.int32)] * K
        dq = [jnp.zeros((8, LANES), F32)] * K
        for b in range(0, n, R):
            p = lax.dot_general(x_ref[b:b + R, :], xt, NT, preferred_element_type=F32)
            for r in range(0, R, 8):
                q = q_ref[b + r:b + r + 8, :]
                for l in range(K):
                    item = p[r:r + 8, l * LANES:(l + 1) * LANES]
                    lo = t + l * LANES
                    on = lo <= b + r < lo + LANES
                    if on:
                        mask = gap == b + r - lo
                        dq[l] = dq[l] + jnp.where(mask, item, 0.0)
                    item = item - q
                    if on:
                        item = jnp.where(mask, LOW, item)
                    g_ref[b + r:b + r + 8, lo:lo + LANES] = item
                    at[l] = jnp.where(item > one[l], b + r, at[l])
                    one[l], two[l] = push(one[l], two[l], item)
        for l in range(K):
            lanes = slice(t + l * LANES, t + (l + 1) * LANES)
            top, next_, a = fold(one[l], two[l], at[l] + sub8)
            own = jnp.broadcast_to(pref[:, lanes] + 0.5 * jnp.sum(dq[l], axis=0, keepdims=True), (8, LANES))
            first, second = push(top, next_, own)
            row_ref[STAR, :, lanes] = top
            row_ref[FIRST, :, lanes] = first
            row_ref[GAIN, :, lanes] = jnp.maximum(0.25 * (top - jnp.maximum(next_, own)), 0.0)
            row_ref[OWN, :, lanes] = own
            row_ref[R1D, :, lanes] = 0.5 * (own - jnp.where(own == first, second, first))
            k_ref[0, :, lanes] = a
            k_ref[1, :, lanes] = a - sub8
    H = -(-blocks // 16) * 16
    subL = lax.broadcasted_iota(jnp.int32, (LANES, LANES), 0)
    subH = lax.broadcasted_iota(jnp.int32, (H, LANES), 0)
    short, diag, tall, eyes = [[], [], []], [[], [], []], [], []
    eye = jnp.where(subL == lax.broadcasted_iota(jnp.int32, (LANES, LANES), 1), 1.0, 0.0).astype(BF16)
    for l in range(blocks):
        lanes = slice(l * LANES, (l + 1) * LANES)
        k = k_ref[0, 0:1, lanes]
        eyes.append(eye)
        for i, part in enumerate(thirds(0.5 * row_ref[R1D, 0:1, lanes])):
            diag[i].append(jnp.where(subH == l, part, 0.0).astype(BF16))
        tall.append(jnp.where(subL == k % LANES, 1.0, 0.0).astype(BF16))
        for i, part in enumerate(thirds(row_ref[GAIN, 0:1, lanes])):
            short[i].append(jnp.where(subH == k // LANES, part, 0.0).astype(BF16))
    tall, eyes = jnp.concatenate(tall, 1), jnp.concatenate(eyes, 1)
    short = jnp.concatenate([jnp.concatenate(s, 1) for s in short], 0)
    diag = jnp.concatenate([jnp.concatenate(s, 1) for s in diag], 0)
    s = lax.dot_general(short, tall, NT, preferred_element_type=F32)
    s = (s[0:H] + s[H:2 * H]) + s[2 * H:]
    side = lax.dot_general(jnp.concatenate([tall, eyes], 1), jnp.concatenate([short, diag], 1), NT, preferred_element_type=F32)
    side = (side[:, 0:H] + side[:, H:2 * H]) + side[:, 2 * H:]
    half = []
    for l in range(blocks):
        lanes = slice(l * LANES, (l + 1) * LANES)
        c = jnp.broadcast_to(side[:, l:l + 1], (LANES, LANES))
        c_ref[:, lanes] = c
        a_ref[:, lanes] = jnp.minimum(c, 0.0)
        av = s[l:l + 1, :]
        row_ref[AV1D, :, lanes] = jnp.broadcast_to(av, (8, LANES))
        half.append(av + 0.5 * row_ref[R1D, 0:1, lanes])
    half = jnp.concatenate(half + [jnp.zeros((H - blocks, LANES), F32)] * (H > blocks), 0)
    half = jnp.concatenate(thirds(half), 0).astype(BF16)
    got = jnp.dot(half, tall, preferred_element_type=F32)
    got = (got[0:H] + got[H:2 * H]) + got[2 * H:]
    for l in range(blocks):
        lanes = slice(l * LANES, (l + 1) * LANES)
        k = k_ref[0, 0:1, lanes]
        c = jnp.sum(jnp.where(subH == k // LANES, got[:, lanes], 0.0), axis=0, keepdims=True)
        row_ref[WZ, :, lanes] = jnp.broadcast_to(c, (8, LANES))
    for t in range(0, n, T):
        K = T // LANES
        lanes = [slice(t + l * LANES, t + (l + 1) * LANES) for l in range(K)]
        star = [k_ref[1, :, k] for k in lanes]
        def tops(j, tops):
            one, two = list(tops[:K]), list(tops[K:])
            base = pl.multiple_of(j * LANES, LANES)
            near = [s - base for s in star]
            for r in range(0, LANES, 8):
                a = a_ref[r:r + 8, pl.ds(base, LANES)]
                for l, k in enumerate(lanes):
                    u = jnp.where(near[l] == r, LOW, g_ref[pl.ds(pl.multiple_of(base + r, 8), 8), k] + a)
                    one[l], two[l] = push(one[l], two[l], u)
            return one + two
        ends = lax.fori_loop(0, blocks, tops, [low8] * (2 * K))
        for l, k in enumerate(lanes):
            row_ref[ONE, :, k], row_ref[TWO, :, k], _ = fold(ends[l], ends[K + l])
    for l in range(blocks):
        k = slice(l * LANES, (l + 1) * LANES)
        one, two = row_ref[ONE, :, k], row_ref[TWO, :, k]
        own, r1d, first, gain, av1d = (row_ref[i, :, k] for i in (OWN, R1D, FIRST, GAIN, AV1D))
        t = jnp.minimum(row_ref[WZ, :, k] - gain, 0.0)
        star = row_ref[STAR, :, k] + t
        own2 = own + av1d
        one, two = push(one, two, star)
        one, two = push(one, two, own2)
        z = (2 / 3) * (one - two)
        row_ref[ONE, :, k] = one
        row_ref[BASE, :, k] = (first + 2.0 * one) * (1 / 3)
        row_ref[Z, :, k] = z
        row_ref[R2D, :, k] = 0.5 * r1d + 0.5 * (own - jnp.where(own2 == one, two, one))
        row_ref[WZ, :, k] = (4 / 3) * gain + jnp.where(star == one, z, 0.0)
        row_ref[STAR, :, k] = t
    r0, c0 = row_idx * rows, col_idx * cols
    off = pl.multiple_of(r0 % LANES, 8)
    w0 = pl.multiple_of((r0 // LANES) * LANES, LANES)
    def block(j):
        st = pl.multiple_of(c0 + j * LANES, LANES)
        groups = LANES // 8
        at = [pl.ds(pl.multiple_of(st + 8 * r, 8), 8) for r in range(groups)]
        a = [a_ref[8 * r:8 * r + 8, pl.ds(st, LANES)] for r in range(groups)]
        r2d = (4 / 3) * row_ref[R2D, :, pl.ds(st, LANES)]
        acc = [jnp.where(gap == 8 * r, r2d, 0.0) for r in range(groups)]
        def resp2(r, k, star, row):
            g = g_ref[at[r], k]
            more = jnp.where(g + a[r] == row[0], row[2], 0.0)
            return (g - row[1]) + jnp.where(star == 8 * r, row[3], more)
        for l in range(blocks):
            k = slice(l * LANES, (l + 1) * LANES)
            star = k_ref[1, :, k] - st
            row = [row_ref[i, :, k] for i in (ONE, BASE, Z, WZ)]
            for r in range(groups):
                acc[r] = acc[r] + jnp.maximum(resp2(r, k, star, row), 0.0)
        cs = [0.375 * jnp.broadcast_to(jnp.sum(v, axis=1, keepdims=True), (8, LANES)) for v in acc]
        for l in range(0, win, LANES):
            k = pl.ds(pl.multiple_of(w0 + l, LANES), LANES)
            star = k_ref[1, :, k] - st
            row = [row_ref[i, :, k] for i in (ONE, BASE, Z, WZ)]
            rd, ad, ts = row_ref[R2D, :, k], row_ref[AV1D, :, k], row_ref[STAR, :, k]
            for r in range(groups):
                r2 = 0.75 * resp2(r, k, star, row)
                t = jnp.where(star == 8 * r, ts, a[r])
                a2 = 0.5 * t + jnp.minimum(cs[r] - 0.5 * jnp.maximum(r2, 0.0), 0.0)
                dg = gap == st + 8 * r - (w0 + l)
                r_out[8 * r:8 * r + 8, j * win + l:j * win + l + LANES] = jnp.where(dg, rd, r2)
                a_out[8 * r:8 * r + 8, j * win + l:j * win + l + LANES] = jnp.where(dg, 0.5 * ad + (cs[r] - 0.5 * rd), a2)
        lanes = slice(j * LANES, (j + 1) * LANES)
        for i, (tile, out_ref) in enumerate(((r_out, resp_ref), (a_out, avail_ref))):
            t_ref[i, :, lanes] = tile[:, j * win:(j + 1) * win].T
            copy = pltpu.make_async_copy(t_ref.at[i, pl.ds(off, rows), lanes], out_ref.at[:, lanes], out_sem.at[j, i])
            copy.start()
            copies.append(copy)
    copies = []
    for j in range(cols // LANES):
        block(j)
    for copy in copies:
        copy.wait()


def early_kernel(mesh_n, mol, owners, *refs):
    me = lax.axis_index("row") * mesh_n[1] + lax.axis_index("col")
    for piece, masks in zip(refs, owners):
        place(mesh_n, mol, me, piece, masks, *refs[-2:])


def compute(pieces, mesh_n, mol, owners, early, rows, cols):
    n, width = mol * mesh_n[0] * mesh_n[1], pieces[0].shape[1]
    win = -(-(rows + LANES - math.gcd(rows, LANES)) // LANES) * LANES
    held = [jax.ShapeDtypeStruct((n, width), BF16), jax.ShapeDtypeStruct((n, LANES), F32)]
    first = pl.pallas_call(
        functools.partial(early_kernel, mesh_n, mol, [owners[i] for i in early]),
        out_shape=held,
        in_specs=[pl.BlockSpec(memory_space=pltpu.VMEM)] * len(early),
        out_specs=[pl.BlockSpec(memory_space=pltpu.VMEM)] * 2,
        cost_estimate=pl.CostEstimate(flops=4 * n * width * LANES, bytes_accessed=4 << 20, transcendentals=0),
        compiler_params=pltpu.CompilerParams(vmem_limit_bytes=40 << 20),
    )(*[pieces[i] for i in early])
    return pl.pallas_call(
        functools.partial(kernel, mesh_n, mol, owners, early, rows, cols, win),
        out_shape=[jax.ShapeDtypeStruct((rows, cols), F32)] * 2 + held,
        in_specs=[pl.BlockSpec(memory_space=pltpu.VMEM)] * (len(pieces) + 2),
        out_specs=[pl.BlockSpec(memory_space=pl.ANY)] * 2 + [pl.BlockSpec(memory_space=pltpu.VMEM)] * 2,
        input_output_aliases={0: 2, 1: 3},
        scratch_shapes=[
            pltpu.VMEM((mesh_n[0], width), F32),
            pltpu.VMEM((n, n), F32),
            pltpu.VMEM((LANES, n), F32),
            pltpu.VMEM((LANES, n), F32),
            pltpu.VMEM((12, 8, n), F32),
            pltpu.VMEM((2, 8, n), jnp.int32),
            pltpu.VMEM((LANES, cols // LANES * win), F32),
            pltpu.VMEM((LANES, cols // LANES * win), F32),
            pltpu.VMEM((2, win, cols), F32),
            pltpu.SemaphoreType.DMA((cols // LANES, 2)),
        ],
        compiler_params=pltpu.CompilerParams(vmem_limit_bytes=40 << 20),
    )(*first, *pieces)[:2]


def pack_kernel(mol, embedding_ref, preference_ref, out_ref, e_ref, p_ref, sems):
    copies = [
        pltpu.make_async_copy(preference_ref, p_ref, sems.at[0]),
        pltpu.make_async_copy(embedding_ref, e_ref, sems.at[1]),
    ]
    for copy in copies:
        copy.start()
    for copy in copies:
        copy.wait()
    out_ref[0:mol, :] = e_ref[...]
    values = p_ref[...]
    high, mid, low = thirds(values)
    odd = lax.axis_index("col") // 2 % 2 == 1
    fill = jnp.zeros((1, out_ref.shape[1] - values.shape[1]), F32)
    one, two = (jnp.concatenate([part, fill], 1) for part in (jnp.where(odd, low, high), jnp.where(odd, 0.0, mid)))
    at = lax.broadcasted_iota(jnp.int32, (8, out_ref.shape[1]), 0) - lax.axis_index("row") // 2 * 2
    out_ref[mol:mol + 8, :] = jnp.where(at == 0, one, jnp.where(at == 1, two, 0.0)).astype(BF16)


def pack(embedding, preference):
    mol, width = embedding.shape
    return pl.pallas_call(
        functools.partial(pack_kernel, mol),
        out_shape=pltpu.VMEM((mol + 8, width), BF16),
        in_specs=[pl.BlockSpec(memory_space=pltpu.HBM)] * 2,
        out_specs=pl.BlockSpec(memory_space=pltpu.VMEM),
        scratch_shapes=[pltpu.VMEM((mol, width), BF16), pltpu.VMEM(preference.shape, F32), pltpu.SemaphoreType.DMA((2,))],
        compiler_params=pltpu.CompilerParams(vmem_limit_bytes=60 << 20),
    )(embedding, preference)


def fits(rows_n, cols_n, mol, width):
    n = mol * rows_n * cols_n
    two = rows_n in (2, 4, 8) and cols_n >= 4 and not cols_n & (cols_n - 1)
    return (two and 4 * n * n <= 16 << 20 and n % 512 == 0 and mol * rows_n % LANES == 0 and mol % 16 == 0
            and mol * cols_n <= width and width % LANES == 0)


def stages(rows_n, cols_n):
    far = [m * 2 * cols_n + 1 for m in range(1,rows_n//2)]
    near = [m * 2 + 1 for m in range(1,cols_n)]
    return far, near


def swap(block, mask):
    size = lax.axis_size("row") * lax.axis_size("col")
    return lax.ppermute(block, ("row", "col"), [(i, i ^ mask) for i in range(size)])


def replicated(embedding, preference):
    rows_n, cols_n = lax.axis_size("row"), lax.axis_size("col")
    mol, width = embedding.shape[2:]
    rows, cols = mol * cols_n, mol * rows_n
    held = pack(embedding.reshape(mol, width), preference.reshape(1, rows))
    far, near = stages(rows_n, cols_n)
    line = [held] + [swap(held, m) for m in far]
    line = jnp.concatenate([h[:mol] for h in line] + [sum(h[mol:] for h in line)], 0)
    pieces = [line] + [swap(line, m) for m in near]
    owners = [[n ^ f for f in [0] + far] for n in [0] + near]
    pieces = pieces + [swap(piece, 1) for piece in pieces]
    owners = owners + [[m ^ 1 for m in masks] for masks in owners]
    early = (*range(len(near) + 2), 2 * len(near) + 1)
    return tuple(compute(pieces, (rows_n, cols_n), mol, owners, early, rows, cols))


def local(embedding, preference):
    if fits(lax.axis_size("row"), lax.axis_size("col"), *embedding.shape[2:]):
        return replicated(embedding, preference)
    return tiled(embedding, preference)


def broadcast(block, axis, source):
    block = jnp.where(lax.axis_index(axis) == source, block, jnp.zeros_like(block))
    return lax.psum(block, axis)


def similarity(row_emb, col_emb, row_start, col_start, pref_rows):
    cross = lax.dot_general(
        row_emb, col_emb, (((1,), (1,)), ((), ())), preferred_element_type=jnp.float32
    )
    row_vals = row_emb.astype(jnp.float32)
    col_vals = col_emb.astype(jnp.float32)
    row_sq = jnp.sum(row_vals * row_vals, axis=1)
    col_sq = jnp.sum(col_vals * col_vals, axis=1)
    dist = 2.0 * cross - row_sq[:, None] - col_sq[None, :]
    row_ids = row_start + jnp.arange(row_emb.shape[0], dtype=jnp.int32)
    col_ids = col_start + jnp.arange(col_emb.shape[0], dtype=jnp.int32)
    diagonal = row_ids[:, None] == col_ids[None, :]
    return (jnp.where(diagonal, pref_rows[:, None], dist), diagonal)


def top_two(summed):
    first = jnp.max(summed, axis=1)
    hits = summed == first[:, None]
    repeats = jnp.sum(hits.astype(jnp.int32), axis=1)
    others = jnp.max(jnp.where(hits, -jnp.inf, summed), axis=1)
    second = jnp.where(repeats > 1, first, others)
    return (first, second)


def tiled(embedding, preference):
    rows_n = lax.axis_size("row")
    cols_n = lax.axis_size("col")
    row_idx = lax.axis_index("row")
    col_idx = lax.axis_index("col")
    mol = embedding.shape[2]
    width = embedding.shape[3]
    row_count = mol * cols_n
    col_count = mol * rows_n
    column_block = lax.all_gather(embedding, "row", axis=1, tiled=True).reshape(col_count, width)
    offset = row_idx * cols_n % rows_n
    root = row_idx * cols_n // rows_n
    own_slice = lax.dynamic_slice_in_dim(column_block, offset * mol, row_count, 0)
    row_block = broadcast(own_slice, "col", root)
    row_start = row_idx * row_count
    col_start = col_idx * col_count
    sim, diagonal = similarity(row_block, column_block, row_start, col_start, preference)
    resp = jnp.zeros_like(sim)
    avail = jnp.zeros_like(sim)
    for step in range(ITERS):
        summed = avail + sim
        local_first, local_second = top_two(summed)
        firsts, seconds = (
            lax.all_gather(local_first, "col", axis=0, tiled=True),
            lax.all_gather(local_second, "col", axis=0, tiled=True),
        )
        firsts = firsts.reshape(cols_n, row_count)
        seconds = seconds.reshape(cols_n, row_count)
        first = jnp.max(firsts, axis=0)
        at_top = firsts == first[None, :]
        repeats = jnp.sum(at_top.astype(jnp.int32), axis=0)
        others = jnp.max(jnp.where(at_top, -jnp.inf, firsts), axis=0)
        second = jnp.where(repeats > 1, first, jnp.maximum(jnp.max(seconds, axis=0), others))
        fresh = sim - jnp.where(summed == first[:, None], second[:, None], first[:, None])
        resp = DAMPING * resp + (1.0 - DAMPING) * fresh
        positive = jnp.where(diagonal, resp, jnp.maximum(resp, 0.0))
        colsum = lax.psum(jnp.sum(positive, axis=0), "row")
        renew = colsum[None, :] - positive
        renew = jnp.where(diagonal, renew, jnp.minimum(renew, 0.0))
        avail = DAMPING * avail + (1.0 - DAMPING) * renew
    return (resp, avail)


def solution(mesh):
    placed = (P("col", "row", None, None), P("row"))
    return jax.shard_map(
        local,
        mesh=mesh,
        in_specs=placed,
        out_specs=(P("row", "col"), P("row", "col")),
        check_vma=False,
    )
```
